256 devices in a mesh: flow: 16 (over y_lo, x, core), span: 16 (over y_hi, z).
Axes of the slice: x: 4, y: 4 (y_hi: 2, y_lo: 2; y = y_hi * 2 + y_lo), z: 8, core: 2. Of those that a mesh axis runs over, the one named last changes fastest.
Arguments:
- populations: float32 [19, 256, 256, 128], P(None, 'flow', 'span'), as said below
- gray: float32 [256, 256, 128], P('flow', 'span'), may hold values from 0 to 0.6
- fluid_mask: int32 [256, 256, 128], P('flow', 'span'), may hold values from 0 to 1, as said below
- cotangent: float32 [19, 256, 256, 128], P(None, 'flow', 'span'), may hold values from -6 to 6
Outputs:
- initial_adjoint: float32 [19, 256, 256, 128], P(None, 'flow', 'span')
- profile: float32 [256], P('flow')
The draws below stay inside these ranges and needn't reach their ends.
Inputs may be any that keep to these rules, and one draw needn't show every extreme that they name: populations are positive, each within 40 percent of an equilibrium at a density of 0.7 to 1.3 with velocity components under 0.1. fluid_mask is 0 throughout rock tiles, the aligned cubes of 16 x 16 x 16 voxels that hold no pore; how many tiles of one device's block hold pore differs from block to block.
All inputs are finite; a program needn't handle non-finite values.
Results may differ from the reference program's by a relative error of at most 0.0003.
Values sent between devices are 32-bit elements; how exact they have to be, the bound alone decides.
A program may use at most 128 MiB of HBM per device.

```python
import math
import jax
import jax.numpy as jnp
import numpy as np
from jax import lax

Q = 19
TILE = 16
CX = 16
CY = 16
NX = 256
NY = 256
NZ = 128


def lattice_velocity_drawn():
    return np.array([[0, 0, 0], [1, 0, 0], [-1, 0, 0], [0, 1, 0], [0, -1, 0], [0, 0, 1], [0, 0, -1], [1, 1, 0], [-1, -1, 0], [1, -1, 0], [-1, 1, 0], [1, 0, 1], [-1, 0, -1], [1, 0, -1], [-1, 0, 1], [0, 1, 1], [0, -1, -1], [0, 1, -1], [0, -1, 1]])


def near_equilibrium(density, flow_speed, noise):
    velocity = lattice_velocity_drawn()
    length = np.sum(velocity * velocity, axis=1)
    weights_q = jnp.asarray(np.where(length == 0, 1.0 / 3.0, np.where(length == 1, 1.0 / 18.0, 1.0 / 36.0)), jnp.float32)
    table = jnp.asarray(velocity, jnp.float32)
    projected = jnp.einsum('ia,axyz->ixyz', table, flow_speed)
    speed_sq = jnp.sum(flow_speed * flow_speed, axis=0)
    base = weights_q[:, None, None, None] * density * (1.0 + 3.0 * projected + 4.5 * projected * projected - 1.5 * speed_sq)
    return (base * (1.0 + noise)).astype(jnp.float32)


def draw_populations(key, part):
    key = jax.random.fold_in(key, 7)
    first, second, third = jax.random.split(key, 3)
    density = jax.random.uniform(first, (NX, NY, NZ), jnp.float32, 0.85, 1.15)
    flow_speed = jax.random.uniform(second, (3, NX, NY, NZ), jnp.float32, -0.05, 0.05)
    noise = jax.random.uniform(third, (19, NX, NY, NZ), jnp.float32, -0.3, 0.3)
    return near_equilibrium(density, flow_speed, noise)


def draw_fluid_mask(key, part):
    key = jax.random.fold_in(key, 11)
    first, second, third = jax.random.split(key, 3)
    tiles_x, tiles_y, tiles_z = (NX // TILE, NY // TILE, NZ // TILE)
    blocks_x, blocks_y = (NX // CX, NY // CY)
    levels = jnp.array([1, 1, 1, 2, 2, 3, 6], jnp.int32)
    block_level = levels[jax.random.randint(first, (blocks_x, blocks_y), 0, 7)]
    tile_level = jnp.repeat(jnp.repeat(block_level, CX // TILE, axis=0), CY // TILE, axis=1)
    active = (jax.random.randint(second, (tiles_x, tiles_y, tiles_z), 0, 8) < tile_level[:, :, None]).astype(jnp.int32)
    active = jnp.repeat(jnp.repeat(jnp.repeat(active, TILE, axis=0), TILE, axis=1), TILE, axis=2)
    voxels = (jax.random.randint(third, (NX, NY, NZ), 0, 5) < 4).astype(jnp.int32)
    return active * voxels


def block_levels(key, dims, cuts, smallest, top_value):
    level, own = 1.0, jax.random.fold_in(key, 6)
    for axis_at, blocks in cuts:
        heights = jnp.exp(jax.random.uniform(jax.random.fold_in(own, axis_at), (blocks,), jnp.float32, smallest / len(cuts), top_value / len(cuts)))
        level = level * jnp.repeat(heights, dims[axis_at] // blocks).reshape([-1 if axis == axis_at else 1 for axis in range(len(dims))])
    return level


def gaussian(key, shape, width, most, cuts=(), dtype=jnp.bfloat16):
    gain = block_levels(key, shape, cuts, -0.22, 0.18) if cuts else 1.0
    drawn = jax.random.normal(key, shape, jnp.float32) * width * gain
    return jnp.minimum(jnp.maximum(drawn, -most), most).astype(dtype)


def setup_inputs(seed: int = 0) -> dict:
    streams_of = jax.random.split(jax.random.key(seed), 5)
    populations = draw_populations(jax.random.fold_in(streams_of[4], 71), 0)
    gray = jnp.clip(0.6 * jax.random.uniform(streams_of[1], (NX, NY, NZ), jnp.float32) ** block_levels(streams_of[1], (NX, NY, NZ), ((0, 16), (1, 16)), -0.2, 0.2), 0.0, 0.6)
    fluid_mask = draw_fluid_mask(jax.random.fold_in(streams_of[4], 71), 0)
    cotangent = gaussian(streams_of[3], (Q, NX, NY, NZ), 1.0, 6.0, ((1, 16), (2, 16)), jnp.float32)
    return dict(populations=populations, gray=gray, fluid_mask=fluid_mask, cotangent=cotangent)


def lattice_velocity():
    return np.array([[0, 0, 0], [1, 0, 0], [-1, 0, 0], [0, 1, 0], [0, -1, 0], [0, 0, 1], [0, 0, -1], [1, 1, 0], [-1, -1, 0], [1, -1, 0], [-1, 1, 0], [1, 0, 1], [-1, 0, -1], [1, 0, -1], [-1, 0, 1], [0, 1, 1], [0, -1, -1], [0, 1, -1], [0, -1, 1]])

def lattice_weights():
    velocity = lattice_velocity()
    length = np.sum(velocity * velocity, axis=1)
    return np.where(length == 0, 1.0 / 3.0, np.where(length == 1, 1.0 / 18.0, 1.0 / 36.0))

def opposite_index():
    velocity = lattice_velocity()
    return np.array([int(np.argmin(np.sum(np.abs(velocity + velocity[i]), axis=1))) for i in range(19)])

def moment_value(order, along_x, along_y, along_z):
    table = [1, along_x, along_y, along_z, along_x * along_x, along_y * along_y, along_z * along_z, along_x * along_y, along_x * along_z, along_y * along_z, along_x * along_x * along_y, along_x * along_x * along_z, along_y * along_y * along_x, along_y * along_y * along_z, along_z * along_z * along_x, along_z * along_z * along_y, along_x * along_x * along_y * along_y, along_x * along_x * along_z * along_z, along_y * along_y * along_z * along_z]
    return 1.0 * table[order]

def relax_matrix():
    velocity = [[int(entry) for entry in row_item] for row_item in lattice_velocity()]
    moments = [[moment_value(order, entry[0], entry[1], entry[2]) for entry in velocity] for order in range(19)]
    rates = [0.0] * 4 + [1.0 / 0.6] * 6 + [1.2] * 9
    augment = [moments[row][:] + [rates[row] * moments[row][col] for col in range(19)] for row in range(19)]
    for col in range(19):
        best = col
        for other in range(col + 1, 19):
            if abs(augment[other][col]) > abs(augment[best][col]):
                best = other
        augment[col], augment[best] = (augment[best], augment[col])
        leading = augment[col][col]
        augment[col] = [entry / leading for entry in augment[col]]
        for row in range(19):
            if row != col:
                factor = augment[row][col]
                augment[row] = [left - factor * right for left, right in zip(augment[row], augment[col])]
    return [row_list[19:] for row_list in augment]

def collide(field, gray, fluid_mask):
    highest = lax.Precision.HIGHEST
    velocity = jnp.asarray(lattice_velocity(), jnp.float32)
    weights_q = jnp.asarray(lattice_weights(), jnp.float32)
    kernel = jnp.asarray(relax_matrix(), jnp.float32)
    density = lax.optimization_barrier(jnp.sum(field, axis=0))
    momentum = jnp.einsum('ia,ixyz->axyz', velocity, field, precision=highest)
    flow_speed = momentum / density
    projected = jnp.einsum('ia,axyz->ixyz', velocity, flow_speed, precision=highest)
    speed_sq = lax.optimization_barrier(jnp.sum(flow_speed * flow_speed, axis=0))
    equilibrium = weights_q[:, None, None, None] * density * (1.0 + 3.0 * projected + 4.5 * projected * projected - 1.5 * speed_sq)
    relaxed = field - jnp.einsum('ij,jxyz->ixyz', kernel, field - equilibrium, precision=highest)
    bounced = field[opposite_index()]
    share = jnp.where(fluid_mask == 1, gray, jnp.float32(1.0))
    return (1.0 - share) * relaxed + share * bounced

def zero_shift(array, step, axis):
    if step == 0:
        return array
    extent = array.shape[axis]
    zeros = jnp.zeros_like(lax.slice_in_dim(array, 0, 1, axis=axis))
    if step > 0:
        return jnp.concatenate([zeros, lax.slice_in_dim(array, 0, extent - 1, axis=axis)], axis=axis)
    return jnp.concatenate([lax.slice_in_dim(array, 1, extent, axis=axis), zeros], axis=axis)

def move_field(field, sign):
    velocity = lattice_velocity()
    moved = []
    for index in range(19):
        part_i = field[index]
        part_i = jnp.roll(part_i, int(sign * velocity[index, 0]), axis=0)
        part_i = zero_shift(part_i, int(sign * velocity[index, 1]), 1)
        part_i = zero_shift(part_i, int(sign * velocity[index, 2]), 2)
        moved.append(part_i)
    return jnp.stack(moved)

def to_blocks(field):
    blocks = NX // CX
    return field.reshape(19, blocks, CX, NY, NZ).transpose(1, 0, 2, 3, 4)

def from_blocks(blocks):
    return blocks.transpose(1, 0, 2, 3, 4).reshape(19, NX, NY, NZ)

def reference(populations, gray, fluid_mask, cotangent):
    blocks = NX // CX
    gray_blocks = gray.reshape(blocks, CX, NY, NZ)
    mask_blocks = fluid_mask.reshape(blocks, CX, NY, NZ)

    def forward_block(items):
        return collide(items[0], items[1], items[2])

    def adjoint_block(items):
        state, gray_b, mask_b, incoming = items
        _, pullback = jax.vjp(lambda f, g: collide(f, g, mask_b), state, gray_b)
        return pullback(incoming)
    start_blocks = to_blocks(populations)
    post = from_blocks(lax.map(forward_block, (start_blocks, gray_blocks, mask_blocks)))
    second = move_field(post, 1)
    adjoint_two = move_field(cotangent, -1)
    adjoint_pre, gray_two = lax.map(adjoint_block, (to_blocks(second), gray_blocks, mask_blocks, to_blocks(adjoint_two)))
    adjoint_one = move_field(from_blocks(adjoint_pre), -1)
    start_adjoint, gray_one = lax.map(adjoint_block, (start_blocks, gray_blocks, mask_blocks, to_blocks(adjoint_one)))
    total = (gray_one + gray_two).reshape(NX, NY, NZ)
    profile = lax.optimization_barrier(jnp.sum(total, axis=(1, 2))) / jnp.float32(math.sqrt(NY * NZ))
    return (from_blocks(start_adjoint), profile)
```

```python
import functools
import math

import jax
import jax.numpy as jnp
from jax import lax
from jax.experimental import pallas as pl
from jax.experimental.pallas import tpu as pltpu
from jax.sharding import PartitionSpec as P

VELOCITY = (
    (0, 0, 0),
    (1, 0, 0), (-1, 0, 0), (0, 1, 0), (0, -1, 0), (0, 0, 1), (0, 0, -1),
    (1, 1, 0), (-1, -1, 0), (1, -1, 0), (-1, 1, 0),
    (1, 0, 1), (-1, 0, -1), (1, 0, -1), (-1, 0, 1),
    (0, 1, 1), (0, -1, -1), (0, 1, -1), (0, -1, 1),
)
ORDER = (1, 7, 9, 11, 13, 2, 8, 10, 12, 14, 0, 3, 4, 5, 6, 15, 16, 17, 18)
SLOT = tuple(ORDER.index(i) for i in range(19))
X_GROUP = {1: 0, -1: 5}
Y_GROUP = {s: tuple(i for i in range(19) if VELOCITY[i][1] == s) for s in (1, -1)}
CORNER = {(1, 1): 7, (-1, -1): 8, (1, -1): 9, (-1, 1): 10}
CORNERS = ((1, 1), (-1, -1), (1, -1), (-1, 1))
PAIRS = ((1, 2), (3, 4), (5, 6), (7, 8), (9, 10), (11, 12), (13, 14), (15, 16), (17, 18))
RATE = 1.0 / 0.6 - 1.2
PITCH = 32
BASE = 8
NX = 16
NY = 16
NZ = 128


def split(f):
    even = [f[p] + f[m] for p, m in PAIRS]
    odd = [f[p] - f[m] for p, m in PAIRS]
    return even, odd


def sums(even, odd):
    plane = [even[3 + 2 * k] + even[4 + 2 * k] for k in range(3)]
    cross = [even[3 + 2 * k] - even[4 + 2 * k] for k in range(3)]
    plus = [odd[3 + 2 * k] + odd[4 + 2 * k] for k in range(3)]
    minus = [odd[3 + 2 * k] - odd[4 + 2 * k] for k in range(3)]
    first = [plus[0] + plus[1], minus[0] + plus[2], minus[1] + minus[2]]
    return plane, cross, first


def state_of(f):
    even, odd = split(f)
    plane, cross, first = sums(even, odd)
    j = [odd[a] + first[a] for a in range(3)]
    second = [even[0] + (plane[0] + plane[1]), even[1] + (plane[0] + plane[2]), even[2] + (plane[1] + plane[2])]
    rho = (f[0] + second[0]) + (even[1] + even[2]) + plane[2]
    inv = 1.0 / rho
    u = [entry * inv for entry in j]
    return even, odd, cross, j, second, rho, u


def join(even, odd):
    out = [None] * 19
    for k, (p, m) in enumerate(PAIRS):
        out[p] = even[k] + odd[k]
        out[m] = even[k] - odd[k]
    return out


def collide(f, share):
    even, odd, cross, j, second, rho, u = state_of(f)
    keep = 1.0 - share
    k_even = 0.6 * share - 0.1
    k_odd = -0.4 * share - 0.1
    square = [j[a] * u[a] for a in range(3)]
    mixed = [j[0] * u[1], j[0] * u[2], j[1] * u[2]]
    base = rho - 1.5 * (square[0] + square[1] + square[2])
    third = rho * (1.0 / 3.0)
    lack = [second[a] - third - square[a] for a in range(3)]
    rest = 0.4 * base + RATE * (lack[0] + lack[1] + lack[2])
    base_axis = base * (1.0 / 15.0)
    base_edge = base * (1.0 / 30.0)
    grown = [0.15 * square[a] for a in range(3)]
    e_parts = [base_axis + 2.0 * grown[a] - (0.5 * RATE) * lack[a] for a in range(3)]
    ends = ((0, 1), (0, 2), (1, 2))
    o_parts = [0.2 * j[a] for a in range(3)]
    half = [0.1 * j[a] for a in range(3)]
    for k, (a, b) in enumerate(ends):
        common = base_edge + (grown[a] + grown[b])
        twist = (5.0 / 12.0) * mixed[k] - (0.25 * RATE) * cross[k]
        e_parts += [common + twist, common - twist]
        o_parts += [half[a] + half[b], half[a] - half[b]]
    out_even = [k_even * even[k] + keep * e_parts[k] for k in range(9)]
    out_odd = [k_odd * odd[k] + keep * o_parts[k] for k in range(9)]
    out = join(out_even, out_odd)
    out[0] = 2.0 * (k_even * f[0]) + keep * rest
    return out


def pull_back(f, g, share):
    even, odd, cross, j, second, rho, u = state_of(f)
    g_even, g_odd = split(g)
    g_plane, g_cross, g_first = sums(g_even, g_odd)
    keep = 1.0 - share
    k_even = 0.6 * share - 0.1
    k_odd = -0.4 * share - 0.1
    ends = ((0, 1), (0, 2), (1, 2))
    g_axes = g_even[0] + g_even[1] + g_even[2]
    g_edges = g_plane[0] + g_plane[1] + g_plane[2]
    weighted = g[0] * (1.0 / 3.0) + g_axes * (1.0 / 18.0) + g_edges * (1.0 / 36.0)
    both = [g_plane[0] + g_plane[1], g_plane[0] + g_plane[2], g_plane[1] + g_plane[2]]
    diag = [0.5 * g_even[a] - g[0] for a in range(3)]
    side = [0.25 * g_cross[k] for k in range(3)]
    flow = [0.2 * g_odd[a] + 0.1 * g_first[a] for a in range(3)]
    shared = 3.6 * weighted
    entry = [0.6 * g_even[a] + 0.3 * both[a] + (2.0 * RATE) * diag[a] - shared for a in range(3)]
    tilt = [(5.0 / 3.0) * side[k] for k in range(3)]
    turn = [
        u[0] * entry[0] + (tilt[0] * u[1] + tilt[1] * u[2]),
        u[1] * entry[1] + (tilt[0] * u[0] + tilt[2] * u[2]),
        u[2] * entry[2] + (tilt[1] * u[0] + tilt[2] * u[1]),
    ]
    scalar = 1.2 * weighted + (RATE / 3.0) * (diag[0] + diag[1] + diag[2])
    half_turn = [0.5 * turn[a] for a in range(3)]
    bar_rho = scalar - (u[0] * half_turn[0] + u[1] * half_turn[1] + u[2] * half_turn[2])
    grade = 1.2 * (g[0] * f[0]) - rho * scalar
    for a in range(3):
        grade = grade - j[a] * (flow[a] + half_turn[a])
    bend = diag[0] * second[0] + diag[1] * second[1] + diag[2] * second[2]
    bend = bend + side[0] * cross[0] + side[1] * cross[1] + side[2] * cross[2]
    dot_even = g_even[0] * even[0]
    dot_odd = g_odd[0] * odd[0]
    for k in range(1, 9):
        dot_even = dot_even + g_even[k] * even[k]
        dot_odd = dot_odd + g_odd[k] * odd[k]
    grade = grade + RATE * bend + (0.6 * dot_even - 0.4 * dot_odd)
    bar_rho = keep * bar_rho
    bar_j = [keep * (flow[a] + turn[a]) for a in range(3)]
    scale = keep * RATE
    diag = [scale * entry_a for entry_a in diag]
    side = [scale * entry_k for entry_k in side]
    e_parts = [bar_rho - diag[a] for a in range(3)]
    o_parts = list(bar_j)
    for k, (a, b) in enumerate(ends):
        common = e_parts[a] - diag[b]
        e_parts += [common - side[k], common + side[k]]
        o_parts += [bar_j[a] + bar_j[b], bar_j[a] - bar_j[b]]
    out = join(
        [k_even * g_even[k] + e_parts[k] for k in range(9)],
        [k_odd * g_odd[k] + o_parts[k] for k in range(9)],
    )
    out[0] = 2.0 * (k_even * g[0]) + bar_rho
    return out, grade


def lane_shift(value, step, lane):
    if step == 0:
        return value
    if step > 0:
        return jnp.where(lane == 0, 0.0, pltpu.roll(value, 1, 1))
    return jnp.where(lane == NZ - 1, 0.0, pltpu.roll(value, NZ - 1, 1))


def kernel(
    flows, spans,
    pop_hbm, gray_hbm, mask_hbm, cot_hbm,
    out_ref, profile_ref,
    pop, gray, mask, post, cot, pre,
    y_send, y_recv, c_recv, grade_sum, rows,
    in_sems, send_sems, recv_sems, row_send, row_recv,
):
    fl = lax.axis_index("flow")
    sp = lax.axis_index("span")
    up = lax.rem(fl + 1, flows)
    down = lax.rem(fl + flows - 1, flows)
    flow_at = {1: up, -1: down}
    span_at = {1: sp + 1, -1: sp - 1}
    inside = {1: sp < spans - 1, -1: sp > 0}

    def target(step_x, step_y):
        return {
            "flow": flow_at[step_x] if step_x else fl,
            "span": span_at[step_y] if step_y else sp,
        }

    loads = [
        pltpu.make_async_copy(pop_hbm, pop, in_sems.at[0]),
        pltpu.make_async_copy(gray_hbm, gray, in_sems.at[1]),
        pltpu.make_async_copy(mask_hbm, mask, in_sems.at[2]),
    ]
    for load in loads:
        load.start()
    cot_loads = [
        pltpu.make_async_copy(
            cot_hbm.at[ORDER[k]], cot.at[k, pl.ds(1, NX), pl.ds(BASE, NY), :], in_sems.at[3 + k]
        )
        for k in range(19)
    ]
    for load in cot_loads:
        load.start()

    barrier = pltpu.get_barrier_semaphore()
    for step in range(1, spans):
        pl.semaphore_signal(barrier, inc=1, device_id={"flow": fl, "span": lax.rem(sp + step, spans)})
    for step_x in (1, -1):
        pl.semaphore_signal(barrier, inc=1, device_id=target(step_x, 0))
        for step_y in (1, -1):

            @pl.when(inside[step_y])
            def _():
                pl.semaphore_signal(barrier, inc=1, device_id=target(step_x, step_y))

    count = spans + 1 + 2 * (sp > 0).astype(jnp.int32) + 2 * (sp < spans - 1).astype(jnp.int32)
    pl.semaphore_wait(barrier, count)

    def remote(src, dst, turn, index, where):
        return pltpu.make_async_remote_copy(
            src_ref=src,
            dst_ref=dst,
            send_sem=send_sems.at[turn, index],
            recv_sem=recv_sems.at[turn, index],
            device_id=where,
        )

    def copies(buf, sign, turn):
        made = []
        for n, step in enumerate((1, -1)):
            first = X_GROUP[sign * step]
            made.append((
                remote(
                    buf.at[pl.ds(first, 5), NX if step > 0 else 1, pl.ds(BASE, NY), :],
                    buf.at[pl.ds(first, 5), 0 if step > 0 else NX + 1, pl.ds(BASE, NY), :],
                    turn, n, target(step, 0),
                ), None, None,
            ))
        for n, step in enumerate((1, -1)):
            made.append((
                remote(y_send.at[turn, n], y_recv.at[turn, n], turn, 2 + n, target(0, step)),
                inside[step], inside[-step],
            ))
        for n, (step_x, step_y) in enumerate(CORNERS):
            slot = SLOT[CORNER[(sign * step_x, sign * step_y)]]
            made.append((
                remote(
                    buf.at[slot, NX if step_x > 0 else 1, pl.ds(BASE + (8 if step_y > 0 else 0), 8), :],
                    c_recv.at[turn, n], turn, 4 + n, target(step_x, step_y),
                ), inside[step_y], inside[-step_y],
            ))
        return made

    def send(buf, sign, turn):
        flat = buf.reshape(19, (NX + 2) * PITCH, NZ)
        for n, step in enumerate((1, -1)):
            row = PITCH + BASE + (NY - 1 if step > 0 else 0)
            for k, i in enumerate(Y_GROUP[sign * step]):
                y_send[turn, n, k] = flat[SLOT[i], pl.ds(row, NX, stride=PITCH), :]
        made = copies(buf, sign, turn)
        for copy, sent, _ in made:
            if sent is None:
                copy.start()
            else:
                pl.when(sent)(copy.start)
        return made

    def receive(made, buf, sign, turn):
        flat = buf.reshape(19, (NX + 2) * PITCH, NZ)
        for copy, _, received in made:
            if received is None:
                copy.wait_recv()
            else:
                pl.when(received)(copy.wait_recv)
        for n, step in enumerate((1, -1)):
            row = PITCH + BASE + (-1 if step > 0 else NY)

            def place(step=step, n=n, row=row, empty=False):
                for k, i in enumerate(Y_GROUP[sign * step]):
                    value = jnp.zeros((NX, NZ), jnp.float32) if empty else y_recv[turn, n, k]
                    flat[SLOT[i], pl.ds(row, NX, stride=PITCH), :] = value
                for m, (step_x, step_y) in enumerate(CORNERS):
                    if step_y != step:
                        continue
                    slot = SLOT[CORNER[(sign * step_x, sign * step_y)]]
                    at = 7 if step_y > 0 else 0
                    corner = jnp.zeros((1, NZ), jnp.float32) if empty else c_recv[turn, m, pl.ds(at, 1), :]
                    plane = 0 if step_x > 0 else NX + 1
                    flat[slot, pl.ds(plane * PITCH + BASE + (-1 if step > 0 else NY), 1), :] = corner

            pl.when(inside[-step])(place)
            pl.when(jnp.logical_not(inside[-step]))(functools.partial(place, empty=True))

    def finish(made):
        for copy, sent, _ in made:
            if sent is None:
                copy.wait_send()
            else:
                pl.when(sent)(copy.wait_send)

    lane = lax.broadcasted_iota(jnp.int32, (8, NZ), 1)

    def share_at(x, h):
        return jnp.where(mask[x, pl.ds(8 * h, 8), :] == 1, gray[x, pl.ds(8 * h, 8), :], 1.0)

    def moved(buf, x, h, sign):
        return [
            buf[
                SLOT[i],
                x + 1 - sign * VELOCITY[i][0],
                pl.ds(BASE + 8 * h - sign * VELOCITY[i][1], 8),
                :,
            ]
            for i in range(19)
        ]

    def store_moved(buf, x, h, values, sign):
        for i in range(19):
            buf[SLOT[i], x + 1, pl.ds(BASE + 8 * h, 8), :] = lane_shift(values[i], sign * VELOCITY[i][2], lane)

    for load in loads:
        load.wait()

    @pl.loop(0, NX)
    def _(x):
        for h in range(2):
            f = [pop[i, x, pl.ds(8 * h, 8), :] for i in range(19)]
            store_moved(post, x, h, collide(f, share_at(x, h)), 1)

    post_copies = send(post, 1, 0)
    for load in cot_loads:
        load.wait()
    cot_copies = send(cot, -1, 1)
    receive(cot_copies, cot, -1, 1)
    receive(post_copies, post, 1, 0)

    @pl.loop(0, NX)
    def _(x):
        total = None
        for h in range(2):
            f = moved(post, x, h, 1)
            g = [lane_shift(value, -VELOCITY[i][2], lane) for i, value in enumerate(moved(cot, x, h, -1))]
            out, grade = pull_back(f, g, share_at(x, h))
            store_moved(pre, x, h, out, -1)
            grade = jnp.where(mask[x, pl.ds(8 * h, 8), :] == 1, grade, 0.0)
            total = grade if total is None else total + grade
        grade_sum[x] = total

    pre_copies = send(pre, -1, 2)
    receive(pre_copies, pre, -1, 2)

    @pl.loop(0, NX)
    def _(x):
        total = grade_sum[x]
        for h in range(2):
            f = [pop[i, x, pl.ds(8 * h, 8), :] for i in range(19)]
            out, grade = pull_back(f, moved(pre, x, h, -1), share_at(x, h))
            for i in range(19):
                out_ref[i, x, pl.ds(8 * h, 8), :] = out[i]
            total = total + jnp.where(mask[x, pl.ds(8 * h, 8), :] == 1, grade, 0.0)
        grade_sum[x] = total

    partial = jnp.sum(grade_sum[...], axis=1)
    partial = jnp.sum(partial, axis=1, keepdims=True)
    wide = (NX, NZ)
    at_row = lax.broadcasted_iota(jnp.int32, wide, 0) == lax.broadcasted_iota(jnp.int32, wide, 1)
    rows[sp] = jnp.sum(jnp.where(at_row, partial, 0.0), axis=0, keepdims=True)
    row_copies = []
    for step in range(1, spans):
        copy = pltpu.make_async_remote_copy(
            src_ref=rows.at[sp],
            dst_ref=rows.at[sp],
            send_sem=row_send.at[step],
            recv_sem=row_recv.at[step],
            device_id={"flow": fl, "span": lax.rem(sp + step, spans)},
        )
        copy.start()
        row_copies.append(copy)
    finish(post_copies)
    finish(cot_copies)
    finish(pre_copies)
    for copy in row_copies:
        copy.wait_recv()
    total = rows[0]
    for step in range(1, spans):
        total = total + rows[step]
    total = total * (1.0 / math.sqrt(spans * NY * NZ))
    profile_ref[...] = total[:, :NX]
    for copy in row_copies:
        copy.wait_send()


def local(flows, spans, populations, gray, fluid_mask, cotangent):
    padded = pltpu.VMEM((19, NX + 2, PITCH, NZ), jnp.float32)
    block = pltpu.VMEM((19, NX, NY, NZ), jnp.float32)
    adjoint, profile = pl.pallas_call(
        functools.partial(kernel, flows, spans),
        out_shape=(
            jax.ShapeDtypeStruct((19, NX, NY, NZ), jnp.float32),
            jax.ShapeDtypeStruct((1, NX), jnp.float32),
        ),
        in_specs=[pl.BlockSpec(memory_space=pl.ANY)] * 4,
        out_specs=(pl.BlockSpec(memory_space=pltpu.VMEM), pl.BlockSpec(memory_space=pltpu.VMEM)),
        scratch_shapes=[
            block,
            pltpu.VMEM((NX, NY, NZ), jnp.float32),
            pltpu.VMEM((NX, NY, NZ), jnp.int32),
            padded,
            padded,
            padded,
            pltpu.VMEM((3, 2, 5, NX, NZ), jnp.float32),
            pltpu.VMEM((3, 2, 5, NX, NZ), jnp.float32),
            pltpu.VMEM((3, 4, 8, NZ), jnp.float32),
            pltpu.VMEM((NX, 8, NZ), jnp.float32),
            pltpu.VMEM((spans, 1, NZ), jnp.float32),
            pltpu.SemaphoreType.DMA((22,)),
            pltpu.SemaphoreType.DMA((3, 8)),
            pltpu.SemaphoreType.DMA((3, 8)),
            pltpu.SemaphoreType.DMA((spans,)),
            pltpu.SemaphoreType.DMA((spans,)),
        ],
        compiler_params=pltpu.CompilerParams(
            collective_id=0, has_side_effects=True, vmem_limit_bytes=44 * 1024 * 1024
        ),
    )(populations, gray, fluid_mask, cotangent)
    return adjoint, profile.reshape(NX)


def solution(mesh):
    placed = (
        P(None, "flow", "span", None),
        P("flow", "span", None),
        P("flow", "span", None),
        P(None, "flow", "span", None),
    )
    return jax.shard_map(
        functools.partial(local, mesh.shape["flow"], mesh.shape["span"]),
        mesh=mesh,
        in_specs=placed,
        out_specs=(P(None, "flow", "span", None), P("flow")),
        check_vma=False,
    )
```

```python
import functools
import math

import jax
import jax.numpy as jnp
from jax import lax
from jax.experimental import pallas as pl
from jax.experimental.pallas import tpu as pltpu
from jax.sharding import PartitionSpec as P

VELOCITY = (
    (0, 0, 0),
    (1, 0, 0), (-1, 0, 0), (0, 1, 0), (0, -1, 0), (0, 0, 1), (0, 0, -1),
    (1, 1, 0), (-1, -1, 0), (1, -1, 0), (-1, 1, 0),
    (1, 0, 1), (-1, 0, -1), (1, 0, -1), (-1, 0, 1),
    (0, 1, 1), (0, -1, -1), (0, 1, -1), (0, -1, 1),
)
ORDER = (1, 7, 9, 11, 13, 2, 8, 10, 12, 14, 0, 3, 4, 5, 6, 15, 16, 17, 18)
SLOT = tuple(ORDER.index(i) for i in range(19))
X_GROUP = {1: 0, -1: 5}
Y_GROUP = {s: tuple(i for i in range(19) if VELOCITY[i][1] == s) for s in (1, -1)}
CORNER = {(1, 1): 7, (-1, -1): 8, (1, -1): 9, (-1, 1): 10}
CORNERS = ((1, 1), (-1, -1), (1, -1), (-1, 1))
PAIRS = ((1, 2), (3, 4), (5, 6), (7, 8), (9, 10), (11, 12), (13, 14), (15, 16), (17, 18))
RATE = 1.0 / 0.6 - 1.2
ENDS = ((0, 1), (0, 2), (1, 2))
Z_DIRS = tuple(i for i in range(19) if VELOCITY[i][2])
PITCH = 32
BASE = 8
NX = 16
NY = 16
NZ = 128
CHUNKS = 4


def split(f):
    even = [f[p] + f[m] for p, m in PAIRS]
    odd = [f[p] - f[m] for p, m in PAIRS]
    return even, odd


def sums(even, odd):
    plane = [even[3 + 2 * k] + even[4 + 2 * k] for k in range(3)]
    cross = [even[3 + 2 * k] - even[4 + 2 * k] for k in range(3)]
    plus = [odd[3 + 2 * k] + odd[4 + 2 * k] for k in range(3)]
    minus = [odd[3 + 2 * k] - odd[4 + 2 * k] for k in range(3)]
    first = [plus[0] + plus[1], minus[0] + plus[2], minus[1] + minus[2]]
    return plane, cross, first


def state_of(f):
    even, odd = split(f)
    plane, cross, first = sums(even, odd)
    j = [odd[a] + first[a] for a in range(3)]
    second = [even[0] + (plane[0] + plane[1]), even[1] + (plane[0] + plane[2]), even[2] + (plane[1] + plane[2])]
    rho = (f[0] + second[0]) + (even[1] + even[2]) + plane[2]
    inv = 1.0 / rho
    u = [entry * inv for entry in j]
    return even, odd, cross, j, second, rho, u


def join(even, odd):
    out = [None] * 19
    for k, (p, m) in enumerate(PAIRS):
        out[p] = even[k] + odd[k]
        out[m] = even[k] - odd[k]
    return out


def collide(f, share, open_voxel):
    even, odd, cross, j, second, rho, u = state_of(f)
    keep = 1.0 - share
    square = [j[a] * u[a] for a in range(3)]
    mixed = [j[0] * u[1], j[0] * u[2], j[1] * u[2]]
    base = rho - 1.5 * (square[0] + square[1] + square[2])
    third = rho * (1.0 / 3.0)
    lack = [second[a] - third - square[a] for a in range(3)]
    rest = 0.4 * base + RATE * (lack[0] + lack[1] + lack[2])
    base_axis = base * (1.0 / 15.0)
    base_edge = base * (1.0 / 30.0)
    grown = [0.15 * square[a] for a in range(3)]
    e_parts = [base_axis + 2.0 * grown[a] - (0.5 * RATE) * lack[a] for a in range(3)]
    o_parts = [0.2 * j[a] for a in range(3)]
    half = [0.1 * j[a] for a in range(3)]
    for k, (a, b) in enumerate(ENDS):
        common = base_edge + (grown[a] + grown[b])
        twist = (5.0 / 12.0) * mixed[k] - (0.25 * RATE) * cross[k]
        e_parts += [common + twist, common - twist]
        o_parts += [half[a] + half[b], half[a] - half[b]]
    drop = join(
        [jnp.where(open_voxel, 0.6 * even[k] - e_parts[k], 0.0) for k in range(9)],
        [jnp.where(open_voxel, -0.4 * odd[k] - o_parts[k], 0.0) for k in range(9)],
    )
    drop[0] = jnp.where(open_voxel, 1.2 * f[0] - rest, 0.0)
    post = [None] * 19
    post[0] = f[0] - keep * drop[0]
    for p, m in PAIRS:
        post[p] = f[m] - keep * drop[p]
        post[m] = f[p] - keep * drop[m]
    return post, drop, u


def pull_back(u, g, share, state=None):
    g_even, g_odd = split(g)
    g_plane, g_cross, g_first = sums(g_even, g_odd)
    keep = 1.0 - share
    k_even = 0.6 * share - 0.1
    k_odd = -0.4 * share - 0.1
    g_axes = g_even[0] + g_even[1] + g_even[2]
    g_edges = g_plane[0] + g_plane[1] + g_plane[2]
    weighted = g[0] * (1.0 / 3.0) + g_axes * (1.0 / 18.0) + g_edges * (1.0 / 36.0)
    both = [g_plane[0] + g_plane[1], g_plane[0] + g_plane[2], g_plane[1] + g_plane[2]]
    diag = [0.5 * g_even[a] - g[0] for a in range(3)]
    side = [0.25 * g_cross[k] for k in range(3)]
    flow = [0.2 * g_odd[a] + 0.1 * g_first[a] for a in range(3)]
    shared = 3.6 * weighted
    entry = [0.6 * g_even[a] + 0.3 * both[a] + (2.0 * RATE) * diag[a] - shared for a in range(3)]
    tilt = [(5.0 / 3.0) * side[k] for k in range(3)]
    turn = [
        u[0] * entry[0] + (tilt[0] * u[1] + tilt[1] * u[2]),
        u[1] * entry[1] + (tilt[0] * u[0] + tilt[2] * u[2]),
        u[2] * entry[2] + (tilt[1] * u[0] + tilt[2] * u[1]),
    ]
    scalar = 1.2 * weighted + (RATE / 3.0) * (diag[0] + diag[1] + diag[2])
    half_turn = [0.5 * turn[a] for a in range(3)]
    bar_rho = scalar - (u[0] * half_turn[0] + u[1] * half_turn[1] + u[2] * half_turn[2])
    grade = None
    if state is not None:
        even, odd, cross, j, second, rho, rest = state
        grade = 1.2 * (g[0] * rest) - rho * scalar
        for a in range(3):
            grade = grade - j[a] * (flow[a] + half_turn[a])
        bend = diag[0] * second[0] + diag[1] * second[1] + diag[2] * second[2]
        bend = bend + (side[0] * cross[0] + side[1] * cross[1] + side[2] * cross[2])
        dot_even = g_even[0] * even[0]
        dot_odd = g_odd[0] * odd[0]
        for k in range(1, 9):
            dot_even = dot_even + g_even[k] * even[k]
            dot_odd = dot_odd + g_odd[k] * odd[k]
        grade = grade + RATE * bend + (0.6 * dot_even - 0.4 * dot_odd)
    bar_rho = keep * bar_rho
    bar_j = [keep * (flow[a] + turn[a]) for a in range(3)]
    scale = keep * RATE
    diag = [scale * entry_a for entry_a in diag]
    side = [scale * entry_k for entry_k in side]
    e_parts = [bar_rho - diag[a] for a in range(3)]
    o_parts = list(bar_j)
    for k, (a, b) in enumerate(ENDS):
        common = e_parts[a] - diag[b]
        e_parts += [common - side[k], common + side[k]]
        o_parts += [bar_j[a] + bar_j[b], bar_j[a] - bar_j[b]]
    out = join(
        [k_even * g_even[k] + e_parts[k] for k in range(9)],
        [k_odd * g_odd[k] + o_parts[k] for k in range(9)],
    )
    out[0] = 2.0 * (k_even * g[0]) + bar_rho
    return out, grade


def lane_shift(value, step, lane):
    if step == 0:
        return value
    if step > 0:
        return jnp.where(lane == 0, 0.0, pltpu.roll(value, 1, 1))
    return jnp.where(lane == NZ - 1, 0.0, pltpu.roll(value, NZ - 1, 1))


class Field:
    def __init__(self, raw, shifted, y_send, y_recv, c_recv, sign, width, sends, recvs):
        self.raw, self.shifted = raw, shifted
        self.flat_raw = raw.reshape(19 * width, (NX + 2) * PITCH, NZ)
        self.flat_shifted = shifted.reshape(len(Z_DIRS) * width, (NX + 2) * PITCH, NZ)
        self.y_send, self.y_recv, self.c_recv = y_send, y_recv, c_recv
        self.sign, self.width, self.sends, self.recvs = sign, width, sends, recvs

    def slot(self, i, part=0):
        return self.width * SLOT[i] + part

    def z_slot(self, i, part=0):
        return self.width * Z_DIRS.index(i) + part

    def pick(self, i, part=0):
        if VELOCITY[i][2]:
            return self.shifted, self.flat_shifted, self.z_slot(i, part)
        return self.raw, self.flat_raw, self.slot(i, part)


def kernel(
    flows, spans,
    pop_hbm, gray_hbm, mask_hbm, cot_hbm,
    out_hbm, profile_ref,
    pop, gray, mask, speed,
    post_raw, post_z, cot_raw, cot_z, pre_raw, pre_z,
    post_ys, post_yr, post_cr, cot_ys, cot_yr, cot_cr, pre_ys, pre_yr, pre_cr,
    grades, y_grades, rows,
    in_sems, out_sem, send_sems, recv_sems, row_send, row_recv,
):
    fl = lax.axis_index("flow")
    sp = lax.axis_index("span")
    up = lax.rem(fl + 1, flows)
    down = lax.rem(fl + flows - 1, flows)
    flow_at = {1: up, -1: down}
    span_at = {1: sp + 1, -1: sp - 1}
    inside = {1: sp < spans - 1, -1: sp > 0}
    post = Field(post_raw, post_z, post_ys, post_yr, post_cr, 1, 2, send_sems.at[0], recv_sems.at[0])
    cot = Field(cot_raw, cot_z, cot_ys, cot_yr, cot_cr, -1, 1, send_sems.at[1], recv_sems.at[1])
    pre = Field(pre_raw, pre_z, pre_ys, pre_yr, pre_cr, -1, 1, send_sems.at[2], recv_sems.at[2])

    def target(step_x, step_y):
        return {
            "flow": flow_at[step_x] if step_x else fl,
            "span": span_at[step_y] if step_y else sp,
        }

    chunk = NX // CHUNKS
    pop_loads = [
        pltpu.make_async_copy(
            pop_hbm.at[:, pl.ds(chunk * c, chunk)], pop.at[:, pl.ds(chunk * c, chunk)], in_sems.at[c]
        )
        for c in range(CHUNKS)
    ]
    side_loads = [
        pltpu.make_async_copy(gray_hbm, gray, in_sems.at[CHUNKS]),
        pltpu.make_async_copy(mask_hbm, mask, in_sems.at[CHUNKS + 1]),
    ]
    cot_loads = [
        pltpu.make_async_copy(
            cot_hbm.at[ORDER[k]], cot_raw.at[k, pl.ds(1, NX), pl.ds(BASE, NY), :], in_sems.at[CHUNKS + 2 + k]
        )
        for k in range(19)
    ]
    pop_loads[0].start()
    for load in side_loads + pop_loads[1:] + cot_loads:
        load.start()

    steps = sorted(range(spans), key=lambda d: min(d, spans - d))
    peers = [(side, step) for step in steps for side in (0, 1, 2) if side or step]

    def peer(side, step):
        return {"flow": (fl, up, down)[side], "span": lax.rem(sp + step, spans) if step else sp}

    barrier = pltpu.get_barrier_semaphore()
    for side, step in peers:
        pl.semaphore_signal(barrier, inc=1, device_id=peer(side, step))

    def copies(field):
        buf, width, sign = field.raw, field.width, field.sign
        made = []

        def remote(src, dst, index, where, sent, received):
            copy = pltpu.make_async_remote_copy(
                src_ref=src,
                dst_ref=dst,
                send_sem=field.sends.at[index],
                recv_sem=field.recvs.at[index],
                device_id=where,
            )
            made.append((copy, sent, received))

        for n, (step_x, step_y) in enumerate(CORNERS):
            slot = field.slot(CORNER[(sign * step_x, sign * step_y)])
            plane = NX if step_x > 0 else 1
            row = BASE + (NY - 8 if step_y > 0 else 0)
            src = buf.at[pl.ds(slot, width), plane, pl.ds(row, 8), :]
            remote(src, field.c_recv.at[n], 4 + n, target(step_x, step_y), inside[step_y], inside[-step_y])
        for n, step in enumerate((1, -1)):
            remote(field.y_send.at[n], field.y_recv.at[n], 2 + n, target(0, step), inside[step], inside[-step])
        for n, step in enumerate((1, -1)):
            group = pl.ds(width * X_GROUP[sign * step], 5 * width)
            src = buf.at[group, NX if step > 0 else 1, pl.ds(BASE, NY), :]
            dst = buf.at[group, 0 if step > 0 else NX + 1, pl.ds(BASE, NY), :]
            remote(src, dst, n, target(step, 0), None, None)
        return made

    def send(field):
        for n, step in enumerate((1, -1)):
            row = PITCH + BASE + (NY - 1 if step > 0 else 0)
            for k, i in enumerate(Y_GROUP[field.sign * step]):
                for part in range(field.width):
                    field.y_send[n, field.width * k + part] = field.flat_raw[
                        field.slot(i, part), pl.ds(row, NX, stride=PITCH), :
                    ]
        made = copies(field)
        for copy, sent, _ in made:
            if sent is None:
                copy.start()
            else:
                pl.when(sent)(copy.start)
        return made

    lane = lax.broadcasted_iota(jnp.int32, (8, NZ), 1)
    wide_lane = lax.broadcasted_iota(jnp.int32, (NX, NZ), 1)
    row_at = lax.broadcasted_iota(jnp.int32, (8, NZ), 0)

    def receive(made, field):
        sign, width = field.sign, field.width
        for copy, _, received in made:
            if received is None:
                copy.wait_recv()
            else:
                pl.when(received)(copy.wait_recv)
        for n, step in enumerate((1, -1)):
            row = PITCH + BASE + (-1 if step > 0 else NY)

            def place(step=step, n=n, row=row, empty=False):
                for k, i in enumerate(Y_GROUP[sign * step]):
                    for part in range(width):
                        _, flat, slot = field.pick(i, part)
                        if empty:
                            value = jnp.zeros((NX, NZ), jnp.float32)
                        else:
                            value = lane_shift(field.y_recv[n, width * k + part], sign * VELOCITY[i][2], wide_lane)
                        flat[slot, pl.ds(row, NX, stride=PITCH), :] = value
                for m, (step_x, step_y) in enumerate(CORNERS):
                    if step_y != step:
                        continue
                    i = CORNER[(sign * step_x, sign * step_y)]
                    at = 7 if step_y > 0 else 0
                    plane = 0 if step_x > 0 else NX + 1
                    for part in range(width):
                        corner = jnp.zeros((1, NZ), jnp.float32) if empty else field.c_recv[m, part, pl.ds(at, 1), :]
                        field.raw[field.slot(i, part), plane, pl.ds(BASE + (-1 if step > 0 else NY), 1), :] = corner

            pl.when(inside[-step])(place)
            pl.when(jnp.logical_not(inside[-step]))(functools.partial(place, empty=True))
        for plane, step in ((0, 1), (NX + 1, -1)):
            for i in Z_DIRS:
                if VELOCITY[i][0] != sign * step:
                    continue
                for part in range(width):
                    for h in range(2):
                        field.shifted[field.z_slot(i, part), plane, pl.ds(BASE + 8 * h, 8), :] = lane_shift(
                            field.raw[field.slot(i, part), plane, pl.ds(BASE + 8 * h, 8), :],
                            sign * VELOCITY[i][2],
                            lane,
                        )

    def finish(made):
        for copy, sent, _ in made:
            if sent is None:
                copy.wait_send()
            else:
                pl.when(sent)(copy.wait_send)

    def shift_own(field):
        @pl.loop(0, NX // 4)
        def _(block):
            for part in range(field.width):
                values = []
                for i in Z_DIRS:
                    for q in range(4):
                        for h in range(2):
                            at = (4 * block + q + 1, pl.ds(BASE + 8 * h, 8))
                            value = field.raw[field.slot(i, part), at[0], at[1], :]
                            values.append((i, at, lane_shift(value, field.sign * VELOCITY[i][2], lane)))
                for i, at, value in values:
                    field.shifted[field.z_slot(i, part), at[0], at[1], :] = value

    def moved(field, tile, part=0):
        kind, at, h = tile
        values = []
        for i in range(19):
            step_x, step_y = field.sign * VELOCITY[i][0], field.sign * VELOCITY[i][1]
            ref, flat, slot = field.pick(i, part)
            if kind == "x":
                values.append(ref[slot, at + 1 - step_x, pl.ds(BASE + 8 * h - step_y, 8), :])
            else:
                start = (8 * h + 1 - step_x) * PITCH + BASE - step_y + at
                values.append(flat[slot, pl.ds(start, 8, stride=PITCH), :])
        return values

    def flat_of(ref):
        shape = ref.shape
        return ref.reshape(*shape[:-3], NX * NY, NZ)

    def own(ref, tile, *lead):
        kind, at, h = tile
        if kind == "x":
            return ref[(*lead, at, pl.ds(8 * h, 8), slice(None))]
        return flat_of(ref)[(*lead, pl.ds(8 * NY * h + at, 8, stride=NY), slice(None))]

    def share_of(tile):
        open_voxel = own(mask, tile) == 1
        return jnp.where(open_voxel, own(gray, tile), 1.0), open_voxel

    def first_half(tile):
        kind, at, h = tile
        f = moved(post, tile)
        even, odd, cross, j, second, rho, u = state_of(f)
        share, open_voxel = share_of(tile)
        out, grade = pull_back(u, moved(cot, tile), share, (even, odd, cross, j, second, rho, f[0]))
        centre = jnp.where(open_voxel, grade, 0.0)
        parts = [centre, None, None]
        for i, (value, drop) in enumerate(zip(out, moved(post, tile, 1))):
            index = (0, 1, 2)[VELOCITY[i][0]]
            term = value * drop
            parts[index] = term if parts[index] is None else parts[index] + term
        for i in range(19):
            if kind == "x":
                pre_raw[pre.slot(i), at + 1, pl.ds(BASE + 8 * h, 8), :] = out[i]
            else:
                start = (8 * h + 1) * PITCH + BASE + at
                pre.flat_raw[pre.slot(i), pl.ds(start, 8, stride=PITCH), :] = out[i]
        return parts

    def second_half(tile):
        kind, at, h = tile
        share, _ = share_of(tile)
        out, _ = pull_back([own(speed, tile, a) for a in range(3)], moved(pre, tile), share)
        for i in range(19):
            if kind == "x":
                pop[i, at, pl.ds(8 * h, 8), :] = out[i]
            else:
                flat_of(pop)[i, pl.ds(8 * NY * h + at, 8, stride=NY), :] = out[i]

    def without_edge(h, value):
        return jnp.where(row_at == 7 * h, 0.0, value)

    for load in side_loads:
        load.wait()

    def first_collision(x):
        for h in range(2):
            tile = ("x", x, h)
            share, open_voxel = share_of(tile)
            made, drop, u = collide([own(pop, tile, i) for i in range(19)], share, open_voxel)
            for i in range(19):
                post_raw[post.slot(i), x + 1, pl.ds(BASE + 8 * h, 8), :] = made[i]
                post_raw[post.slot(i, 1), x + 1, pl.ds(BASE + 8 * h, 8), :] = drop[i]
            for a in range(3):
                speed[a, x, pl.ds(8 * h, 8), :] = u[a]

    for c in range(CHUNKS):
        if c == CHUNKS - 1:
            pl.semaphore_wait(barrier, len(peers))
            for load in cot_loads:
                load.wait()
            cot_copies = send(cot)
        pop_loads[c].wait()

        @pl.loop(chunk * c, chunk * (c + 1))
        def _(x):
            first_collision(x)

    post_copies = send(post)
    shift_own(post)
    shift_own(cot)

    @pl.loop(1, NX - 1)
    def _(x):
        halves = [[without_edge(h, part) for part in first_half(("x", x, h))] for h in range(2)]
        for q in range(3):
            grades[q, x] = halves[0][q] + halves[1][q]

    receive(cot_copies, cot)
    receive(post_copies, post)

    @pl.loop(0, 2)
    def _(end):
        at = (NX - 1) * end
        halves = [first_half(("x", at, h)) for h in range(2)]
        for q in range(3):
            grades[q, at] = halves[0][q] + halves[1][q]
        for h in range(2):
            for q, part in enumerate(first_half(("y", at, h))):
                y_grades[end, q, pl.ds(8 * h, 8), :] = without_edge(h, part)

    pre_copies = send(pre)

    line = None
    row_index = lax.broadcasted_iota(jnp.int32, (NX, NZ), 0)
    for q, lead in enumerate((1, 0, 2)):
        part = jnp.sum(grades[q], axis=1) + (y_grades[0, q] + y_grades[1, q])
        part = jnp.sum(part, axis=1, keepdims=True)
        part = jnp.where(wide_lane == row_index + lead, part, 0.0)
        line = part if line is None else line + part
    rows[0, sp] = jnp.sum(line, axis=0, keepdims=True)
    row_copies = []
    for side, step in peers:
        copy = pltpu.make_async_remote_copy(
            src_ref=rows.at[0, sp],
            dst_ref=rows.at[side, sp],
            send_sem=row_send.at[side, step],
            recv_sem=row_recv.at[side, step],
            device_id=peer(side, step),
        )
        copy.start()
        row_copies.append(copy)

    shift_own(pre)

    @pl.loop(1, NX - 1)
    def _(x):
        for h in range(2):
            second_half(("x", x, h))

    receive(pre_copies, pre)

    @pl.loop(0, 2)
    def _(end):
        at = (NX - 1) * end
        for h in range(2):
            second_half(("x", at, h))
        for h in range(2):
            second_half(("y", at, h))

    out_copy = pltpu.make_async_copy(pop, out_hbm, out_sem)
    out_copy.start()
    finish(post_copies)
    finish(cot_copies)
    finish(pre_copies)
    for copy in row_copies:
        copy.wait_recv()
    one_lane = lax.broadcasted_iota(jnp.int32, (1, NZ), 1)
    total = jnp.sum(rows[0], axis=0)
    from_down = jnp.sum(rows[1], axis=0)
    from_up = jnp.sum(rows[2], axis=0)
    total = total + jnp.where(one_lane == 1, pltpu.roll(from_down, NZ - NX, 1), 0.0)
    total = total + jnp.where(one_lane == NX, pltpu.roll(from_up, NX, 1), 0.0)
    total = pltpu.roll(total, NZ - 1, 1) * (1.0 / math.sqrt(spans * NY * NZ))
    profile_ref[...] = total[:, :NX]
    for copy in row_copies:
        copy.wait_send()
    out_copy.wait()


def local(flows, spans, populations, gray, fluid_mask, cotangent):
    def vmem(*shape):
        return pltpu.VMEM(shape, jnp.float32)

    zs = len(Z_DIRS)
    faces = [vmem(2, 10, NX, NZ), vmem(2, 10, NX, NZ), vmem(4, 2, 8, NZ)]
    for _ in range(2):
        faces += [vmem(2, 5, NX, NZ), vmem(2, 5, NX, NZ), vmem(4, 1, 8, NZ)]
    adjoint, profile = pl.pallas_call(
        functools.partial(kernel, flows, spans),
        out_shape=(
            jax.ShapeDtypeStruct((19, NX, NY, NZ), jnp.float32),
            jax.ShapeDtypeStruct((1, NX), jnp.float32),
        ),
        in_specs=[pl.BlockSpec(memory_space=pl.ANY)] * 4,
        out_specs=(pl.BlockSpec(memory_space=pl.ANY), pl.BlockSpec(memory_space=pltpu.VMEM)),
        scratch_shapes=[
            vmem(19, NX, NY, NZ),
            vmem(NX, NY, NZ),
            pltpu.VMEM((NX, NY, NZ), jnp.int32),
            vmem(3, NX, NY, NZ),
            vmem(38, NX + 2, PITCH, NZ),
            vmem(2 * zs, NX + 2, PITCH, NZ),
            vmem(19, NX + 2, PITCH, NZ),
            vmem(zs, NX + 2, PITCH, NZ),
            vmem(19, NX + 2, PITCH, NZ),
            vmem(zs, NX + 2, PITCH, NZ),
            *faces,
            vmem(3, NX, 8, NZ),
            vmem(2, 3, NX, NZ),
            vmem(3, spans, 1, NZ),
            pltpu.SemaphoreType.DMA((CHUNKS + 21,)),
            pltpu.SemaphoreType.DMA,
            pltpu.SemaphoreType.DMA((3, 8)),
            pltpu.SemaphoreType.DMA((3, 8)),
            pltpu.SemaphoreType.DMA((3, spans)),
            pltpu.SemaphoreType.DMA((3, spans)),
        ],
        compiler_params=pltpu.CompilerParams(
            collective_id=0, has_side_effects=True, vmem_limit_bytes=60 * 1024 * 1024
        ),
    )(populations, gray, fluid_mask, cotangent)
    return adjoint, profile.reshape(NX)


def solution(mesh):
    placed = (
        P(None, "flow", "span", None),
        P("flow", "span", None),
        P("flow", "span", None),
        P(None, "flow", "span", None),
    )
    return jax.shard_map(
        functools.partial(local, mesh.shape["flow"], mesh.shape["span"]),
        mesh=mesh,
        in_specs=placed,
        out_specs=(P(None, "flow", "span", None), P("flow")),
        check_vma=False,
    )
```

```python
import functools
import math

import jax
import jax.numpy as jnp
from jax import lax
from jax.experimental import pallas as pl
from jax.experimental.pallas import tpu as pltpu
from jax.sharding import PartitionSpec as P

VELOCITY = (
    (0, 0, 0),
    (1, 0, 0), (-1, 0, 0), (0, 1, 0), (0, -1, 0), (0, 0, 1), (0, 0, -1),
    (1, 1, 0), (-1, -1, 0), (1, -1, 0), (-1, 1, 0),
    (1, 0, 1), (-1, 0, -1), (1, 0, -1), (-1, 0, 1),
    (0, 1, 1), (0, -1, -1), (0, 1, -1), (0, -1, 1),
)
ORDER = (1, 7, 9, 11, 13, 2, 8, 10, 12, 14, 0, 3, 4, 5, 6, 15, 16, 17, 18)
SLOT = tuple(ORDER.index(i) for i in range(19))
X_GROUP = {1: 0, -1: 5}
Y_GROUP = {s: tuple(i for i in range(19) if VELOCITY[i][1] == s) for s in (1, -1)}
CORNER = {(1, 1): 7, (-1, -1): 8, (1, -1): 9, (-1, 1): 10}
CORNERS = ((1, 1), (-1, -1), (1, -1), (-1, 1))
PAIRS = ((1, 2), (3, 4), (5, 6), (7, 8), (9, 10), (11, 12), (13, 14), (15, 16), (17, 18))
RATE = 1.0 / 0.6 - 1.2
ENDS = ((0, 1), (0, 2), (1, 2))
Z_DIRS = tuple(i for i in range(19) if VELOCITY[i][2])
PITCH = 32
BASE = 8
NX = 16
NY = 16
NZ = 128
CHUNKS = 4


def split(f):
    even = [f[p] + f[m] for p, m in PAIRS]
    odd = [f[p] - f[m] for p, m in PAIRS]
    return even, odd


def sums(even, odd):
    plane = [even[3 + 2 * k] + even[4 + 2 * k] for k in range(3)]
    cross = [even[3 + 2 * k] - even[4 + 2 * k] for k in range(3)]
    plus = [odd[3 + 2 * k] + odd[4 + 2 * k] for k in range(3)]
    minus = [odd[3 + 2 * k] - odd[4 + 2 * k] for k in range(3)]
    first = [plus[0] + plus[1], minus[0] + plus[2], minus[1] + minus[2]]
    return plane, cross, first


def state_of(f):
    even, odd = split(f)
    plane, cross, first = sums(even, odd)
    j = [odd[a] + first[a] for a in range(3)]
    second = [even[0] + (plane[0] + plane[1]), even[1] + (plane[0] + plane[2]), even[2] + (plane[1] + plane[2])]
    rho = (f[0] + second[0]) + (even[1] + even[2]) + plane[2]
    inv = 1.0 / rho
    u = [entry * inv for entry in j]
    return even, odd, cross, j, second, rho, u


def join(even, odd):
    out = [None] * 19
    for k, (p, m) in enumerate(PAIRS):
        out[p] = even[k] + odd[k]
        out[m] = even[k] - odd[k]
    return out


def collide(f, share, open_voxel):
    even, odd, cross, j, second, rho, u = state_of(f)
    keep = 1.0 - share
    square = [j[a] * u[a] for a in range(3)]
    mixed = [j[0] * u[1], j[0] * u[2], j[1] * u[2]]
    base = rho - 1.5 * (square[0] + square[1] + square[2])
    third = rho * (1.0 / 3.0)
    lack = [second[a] - third - square[a] for a in range(3)]
    rest = 0.4 * base + RATE * (lack[0] + lack[1] + lack[2])
    base_axis = base * (1.0 / 15.0)
    base_edge = base * (1.0 / 30.0)
    grown = [0.15 * square[a] for a in range(3)]
    e_parts = [base_axis + 2.0 * grown[a] - (0.5 * RATE) * lack[a] for a in range(3)]
    o_parts = [0.2 * j[a] for a in range(3)]
    half = [0.1 * j[a] for a in range(3)]
    for k, (a, b) in enumerate(ENDS):
        common = base_edge + (grown[a] + grown[b])
        twist = (5.0 / 12.0) * mixed[k] - (0.25 * RATE) * cross[k]
        e_parts += [common + twist, common - twist]
        o_parts += [half[a] + half[b], half[a] - half[b]]
    drop = join(
        [jnp.where(open_voxel, 0.6 * even[k] - e_parts[k], 0.0) for k in range(9)],
        [jnp.where(open_voxel, -0.4 * odd[k] - o_parts[k], 0.0) for k in range(9)],
    )
    drop[0] = jnp.where(open_voxel, 1.2 * f[0] - rest, 0.0)
    post = [None] * 19
    post[0] = f[0] - keep * drop[0]
    for p, m in PAIRS:
        post[p] = f[m] - keep * drop[p]
        post[m] = f[p] - keep * drop[m]
    return post, drop, u


def pull_back(u, g, share, state=None):
    g_even, g_odd = split(g)
    g_plane, g_cross, g_first = sums(g_even, g_odd)
    keep = 1.0 - share
    k_even = 0.6 * share - 0.1
    k_odd = -0.4 * share - 0.1
    g_axes = g_even[0] + g_even[1] + g_even[2]
    g_edges = g_plane[0] + g_plane[1] + g_plane[2]
    weighted = g[0] * (1.0 / 3.0) + g_axes * (1.0 / 18.0) + g_edges * (1.0 / 36.0)
    both = [g_plane[0] + g_plane[1], g_plane[0] + g_plane[2], g_plane[1] + g_plane[2]]
    diag = [0.5 * g_even[a] - g[0] for a in range(3)]
    side = [0.25 * g_cross[k] for k in range(3)]
    flow = [0.2 * g_odd[a] + 0.1 * g_first[a] for a in range(3)]
    shared = 3.6 * weighted
    entry = [0.6 * g_even[a] + 0.3 * both[a] + (2.0 * RATE) * diag[a] - shared for a in range(3)]
    tilt = [(5.0 / 3.0) * side[k] for k in range(3)]
    turn = [
        u[0] * entry[0] + (tilt[0] * u[1] + tilt[1] * u[2]),
        u[1] * entry[1] + (tilt[0] * u[0] + tilt[2] * u[2]),
        u[2] * entry[2] + (tilt[1] * u[0] + tilt[2] * u[1]),
    ]
    scalar = 1.2 * weighted + (RATE / 3.0) * (diag[0] + diag[1] + diag[2])
    half_turn = [0.5 * turn[a] for a in range(3)]
    bar_rho = scalar - (u[0] * half_turn[0] + u[1] * half_turn[1] + u[2] * half_turn[2])
    grade = None
    if state is not None:
        even, odd, cross, j, second, rho, rest = state
        grade = 1.2 * (g[0] * rest) - rho * scalar
        for a in range(3):
            grade = grade - j[a] * (flow[a] + half_turn[a])
        bend = diag[0] * second[0] + diag[1] * second[1] + diag[2] * second[2]
        bend = bend + (side[0] * cross[0] + side[1] * cross[1] + side[2] * cross[2])
        dot_even = g_even[0] * even[0]
        dot_odd = g_odd[0] * odd[0]
        for k in range(1, 9):
            dot_even = dot_even + g_even[k] * even[k]
            dot_odd = dot_odd + g_odd[k] * odd[k]
        grade = grade + RATE * bend + (0.6 * dot_even - 0.4 * dot_odd)
    bar_rho = keep * bar_rho
    bar_j = [keep * (flow[a] + turn[a]) for a in range(3)]
    scale = keep * RATE
    diag = [scale * entry_a for entry_a in diag]
    side = [scale * entry_k for entry_k in side]
    e_parts = [bar_rho - diag[a] for a in range(3)]
    o_parts = list(bar_j)
    for k, (a, b) in enumerate(ENDS):
        common = e_parts[a] - diag[b]
        e_parts += [common - side[k], common + side[k]]
        o_parts += [bar_j[a] + bar_j[b], bar_j[a] - bar_j[b]]
    out = join(
        [k_even * g_even[k] + e_parts[k] for k in range(9)],
        [k_odd * g_odd[k] + o_parts[k] for k in range(9)],
    )
    out[0] = 2.0 * (k_even * g[0]) + bar_rho
    return out, grade


def lane_shift(value, step, lane):
    if step == 0:
        return value
    if step > 0:
        return jnp.where(lane == 0, 0.0, pltpu.roll(value, 1, 1))
    return jnp.where(lane == NZ - 1, 0.0, pltpu.roll(value, NZ - 1, 1))


class Field:
    def __init__(self, raw, shifted, y_send, y_recv, c_recv, sign, width, sends, recvs):
        self.raw, self.shifted = raw, shifted
        self.flat_raw = raw.reshape(19 * width, (NX + 2) * PITCH, NZ)
        self.flat_shifted = shifted.reshape(len(Z_DIRS) * width, (NX + 2) * PITCH, NZ)
        self.y_send, self.y_recv, self.c_recv = y_send, y_recv, c_recv
        self.sign, self.width, self.sends, self.recvs = sign, width, sends, recvs

    def slot(self, i, part=0):
        return self.width * SLOT[i] + part

    def z_slot(self, i, part=0):
        return self.width * Z_DIRS.index(i) + part

    def pick(self, i, part=0):
        if VELOCITY[i][2]:
            return self.shifted, self.flat_shifted, self.z_slot(i, part)
        return self.raw, self.flat_raw, self.slot(i, part)


def kernel(
    flows, spans,
    pop_hbm, gray_hbm, mask_hbm, cot_hbm,
    out_ref, profile_ref,
    pop, gray, mask, speed,
    post_raw, post_z, cot_raw, cot_z, pre_raw, pre_z,
    post_ys, post_yr, post_cr, cot_ys, cot_yr, cot_cr, pre_ys, pre_yr, pre_cr,
    grades, y_grades, rows,
    in_sems, send_sems, recv_sems, row_send, row_recv,
):
    fl = lax.axis_index("flow")
    sp = lax.axis_index("span")
    up = lax.rem(fl + 1, flows)
    down = lax.rem(fl + flows - 1, flows)
    flow_at = {1: up, -1: down}
    span_at = {1: sp + 1, -1: sp - 1}
    inside = {1: sp < spans - 1, -1: sp > 0}
    post = Field(post_raw, post_z, post_ys, post_yr, post_cr, 1, 2, send_sems.at[0], recv_sems.at[0])
    cot = Field(cot_raw, cot_z, cot_ys, cot_yr, cot_cr, -1, 1, send_sems.at[1], recv_sems.at[1])
    pre = Field(pre_raw, pre_z, pre_ys, pre_yr, pre_cr, -1, 1, send_sems.at[2], recv_sems.at[2])

    def target(step_x, step_y):
        return {
            "flow": flow_at[step_x] if step_x else fl,
            "span": span_at[step_y] if step_y else sp,
        }

    chunk = NX // CHUNKS
    pop_loads = [
        pltpu.make_async_copy(
            pop_hbm.at[:, pl.ds(chunk * c, chunk)], pop.at[:, pl.ds(chunk * c, chunk)], in_sems.at[c]
        )
        for c in range(CHUNKS)
    ]
    side_loads = [
        pltpu.make_async_copy(gray_hbm, gray, in_sems.at[CHUNKS]),
        pltpu.make_async_copy(mask_hbm, mask, in_sems.at[CHUNKS + 1]),
    ]
    cot_loads = [
        pltpu.make_async_copy(
            cot_hbm.at[ORDER[k]], cot_raw.at[k, pl.ds(1, NX), pl.ds(BASE, NY), :], in_sems.at[CHUNKS + 2 + k]
        )
        for k in range(19)
    ]
    pop_loads[0].start()
    for load in side_loads + pop_loads[1:] + cot_loads:
        load.start()

    steps = sorted(range(spans), key=lambda d: min(d, spans - d))
    peers = [(side, step) for step in steps for side in (0, 1, 2) if side or step]

    def peer(side, step):
        return {"flow": (fl, up, down)[side], "span": lax.rem(sp + step, spans) if step else sp}

    barrier = pltpu.get_barrier_semaphore()
    for side, step in peers:
        pl.semaphore_signal(barrier, inc=1, device_id=peer(side, step))

    def copies(field):
        buf, width, sign = field.raw, field.width, field.sign
        made = []

        def remote(src, dst, index, where, sent, received):
            copy = pltpu.make_async_remote_copy(
                src_ref=src,
                dst_ref=dst,
                send_sem=field.sends.at[index],
                recv_sem=field.recvs.at[index],
                device_id=where,
            )
            made.append((copy, sent, received))

        for n, (step_x, step_y) in enumerate(CORNERS):
            slot = field.slot(CORNER[(sign * step_x, sign * step_y)])
            plane = NX if step_x > 0 else 1
            row = BASE + (NY - 8 if step_y > 0 else 0)
            src = buf.at[pl.ds(slot, width), plane, pl.ds(row, 8), :]
            remote(src, field.c_recv.at[n], 4 + n, target(step_x, step_y), inside[step_y], inside[-step_y])
        for n, step in enumerate((1, -1)):
            remote(field.y_send.at[n], field.y_recv.at[n], 2 + n, target(0, step), inside[step], inside[-step])
        for n, step in enumerate((1, -1)):
            group = pl.ds(width * X_GROUP[sign * step], 5 * width)
            src = buf.at[group, NX if step > 0 else 1, pl.ds(BASE, NY), :]
            dst = buf.at[group, 0 if step > 0 else NX + 1, pl.ds(BASE, NY), :]
            remote(src, dst, n, target(step, 0), None, None)
        return made

    def pack(field):
        for n, step in enumerate((1, -1)):
            row = PITCH + BASE + (NY - 1 if step > 0 else 0)
            for k, i in enumerate(Y_GROUP[field.sign * step]):
                for part in range(field.width):
                    field.y_send[n, field.width * k + part] = field.flat_raw[
                        field.slot(i, part), pl.ds(row, NX, stride=PITCH), :
                    ]

    def send(*fields):
        made = [copies(field) for field in fields]
        for several in zip(*made):
            for copy, sent, _ in several:
                if sent is None:
                    copy.start()
                else:
                    pl.when(sent)(copy.start)
        return made

    lane = lax.broadcasted_iota(jnp.int32, (8, NZ), 1)
    wide_lane = lax.broadcasted_iota(jnp.int32, (NX, NZ), 1)
    row_at = lax.broadcasted_iota(jnp.int32, (8, NZ), 0)

    def receive(made, field):
        sign, width = field.sign, field.width
        for copy, _, received in made:
            if received is None:
                copy.wait_recv()
            else:
                pl.when(received)(copy.wait_recv)
        for n, step in enumerate((1, -1)):
            row = PITCH + BASE + (-1 if step > 0 else NY)

            def place(step=step, n=n, row=row, empty=False):
                for k, i in enumerate(Y_GROUP[sign * step]):
                    for part in range(width):
                        _, flat, slot = field.pick(i, part)
                        if empty:
                            value = jnp.zeros((NX, NZ), jnp.float32)
                        else:
                            value = lane_shift(field.y_recv[n, width * k + part], sign * VELOCITY[i][2], wide_lane)
                        flat[slot, pl.ds(row, NX, stride=PITCH), :] = value
                for m, (step_x, step_y) in enumerate(CORNERS):
                    if step_y != step:
                        continue
                    i = CORNER[(sign * step_x, sign * step_y)]
                    at = 7 if step_y > 0 else 0
                    plane = 0 if step_x > 0 else NX + 1
                    for part in range(width):
                        corner = jnp.zeros((1, NZ), jnp.float32) if empty else field.c_recv[m, part, pl.ds(at, 1), :]
                        field.raw[field.slot(i, part), plane, pl.ds(BASE + (-1 if step > 0 else NY), 1), :] = corner

            pl.when(inside[-step])(place)
            pl.when(jnp.logical_not(inside[-step]))(functools.partial(place, empty=True))
        for plane, step in ((0, 1), (NX + 1, -1)):
            for i in Z_DIRS:
                if VELOCITY[i][0] != sign * step:
                    continue
                for part in range(width):
                    for h in range(2):
                        field.shifted[field.z_slot(i, part), plane, pl.ds(BASE + 8 * h, 8), :] = lane_shift(
                            field.raw[field.slot(i, part), plane, pl.ds(BASE + 8 * h, 8), :],
                            sign * VELOCITY[i][2],
                            lane,
                        )

    def finish(made):
        for copy, sent, _ in made:
            if sent is None:
                copy.wait_send()
            else:
                pl.when(sent)(copy.wait_send)

    def shift_own(field):
        @pl.loop(0, NX // 4)
        def _(block):
            for part in range(field.width):
                values = []
                for i in Z_DIRS:
                    for q in range(4):
                        for h in range(2):
                            at = (4 * block + q + 1, pl.ds(BASE + 8 * h, 8))
                            value = field.raw[field.slot(i, part), at[0], at[1], :]
                            values.append((i, at, lane_shift(value, field.sign * VELOCITY[i][2], lane)))
                for i, at, value in values:
                    field.shifted[field.z_slot(i, part), at[0], at[1], :] = value

    def moved(field, tile, part=0):
        kind, at, h = tile
        values = []
        for i in range(19):
            step_x, step_y = field.sign * VELOCITY[i][0], field.sign * VELOCITY[i][1]
            ref, flat, slot = field.pick(i, part)
            if kind == "x":
                values.append(ref[slot, at + 1 - step_x, pl.ds(BASE + 8 * h - step_y, 8), :])
            else:
                start = (8 * h + 1 - step_x) * PITCH + BASE - step_y + at
                values.append(flat[slot, pl.ds(start, 8, stride=PITCH), :])
        return values

    def flat_of(ref):
        shape = ref.shape
        return ref.reshape(*shape[:-3], NX * NY, NZ)

    def own(ref, tile, *lead):
        kind, at, h = tile
        if kind == "x":
            return ref[(*lead, at, pl.ds(8 * h, 8), slice(None))]
        return flat_of(ref)[(*lead, pl.ds(8 * NY * h + at, 8, stride=NY), slice(None))]

    def share_of(tile):
        open_voxel = own(mask, tile) == 1
        return jnp.where(open_voxel, own(gray, tile), 1.0), open_voxel

    def first_half(tile):
        kind, at, h = tile
        f = moved(post, tile)
        even, odd, cross, j, second, rho, u = state_of(f)
        share, open_voxel = share_of(tile)
        out, grade = pull_back(u, moved(cot, tile), share, (even, odd, cross, j, second, rho, f[0]))
        centre = jnp.where(open_voxel, grade, 0.0)
        parts = [centre, None, None]
        for i, (value, drop) in enumerate(zip(out, moved(post, tile, 1))):
            index = (0, 1, 2)[VELOCITY[i][0]]
            term = value * drop
            parts[index] = term if parts[index] is None else parts[index] + term
        for i in range(19):
            if kind == "x":
                pre_raw[pre.slot(i), at + 1, pl.ds(BASE + 8 * h, 8), :] = out[i]
            else:
                start = (8 * h + 1) * PITCH + BASE + at
                pre.flat_raw[pre.slot(i), pl.ds(start, 8, stride=PITCH), :] = out[i]
        return parts

    def second_half(tile):
        kind, at, h = tile
        share, _ = share_of(tile)
        out, _ = pull_back([own(speed, tile, a) for a in range(3)], moved(pre, tile), share)
        for i in range(19):
            if kind == "x":
                out_ref[i, at, pl.ds(8 * h, 8), :] = out[i]
            else:
                flat_of(out_ref)[i, pl.ds(8 * NY * h + at, 8, stride=NY), :] = out[i]

    def without_edge(h, value):
        return jnp.where(row_at == 7 * h, 0.0, value)

    for load in side_loads:
        load.wait()

    def first_collision(x):
        for h in range(2):
            tile = ("x", x, h)
            share, open_voxel = share_of(tile)
            made, drop, u = collide([own(pop, tile, i) for i in range(19)], share, open_voxel)
            for i in range(19):
                post_raw[post.slot(i), x + 1, pl.ds(BASE + 8 * h, 8), :] = made[i]
                post_raw[post.slot(i, 1), x + 1, pl.ds(BASE + 8 * h, 8), :] = drop[i]
            for a in range(3):
                speed[a, x, pl.ds(8 * h, 8), :] = u[a]

    for c in range(CHUNKS):
        pop_loads[c].wait()

        @pl.loop(chunk * c, chunk * (c + 1))
        def _(x):
            first_collision(x)

    pack(post)
    for load in cot_loads:
        load.wait()
    pack(cot)
    pl.semaphore_wait(barrier, len(peers))
    post_copies, cot_copies = send(post, cot)
    shift_own(post)
    shift_own(cot)

    @pl.loop(1, NX - 1)
    def _(x):
        halves = [[without_edge(h, part) for part in first_half(("x", x, h))] for h in range(2)]
        for q in range(3):
            grades[q, x] = halves[0][q] + halves[1][q]

    receive(cot_copies, cot)
    receive(post_copies, post)

    @pl.loop(0, 2)
    def _(end):
        at = (NX - 1) * end
        halves = [first_half(("x", at, h)) for h in range(2)]
        for q in range(3):
            grades[q, at] = halves[0][q] + halves[1][q]
        for h in range(2):
            for q, part in enumerate(first_half(("y", at, h))):
                y_grades[end, q, pl.ds(8 * h, 8), :] = without_edge(h, part)

    pack(pre)
    (pre_copies,) = send(pre)

    line = None
    row_index = lax.broadcasted_iota(jnp.int32, (NX, NZ), 0)
    for q, lead in enumerate((1, 0, 2)):
        part = jnp.sum(grades[q], axis=1) + (y_grades[0, q] + y_grades[1, q])
        part = jnp.sum(part, axis=1, keepdims=True)
        part = jnp.where(wide_lane == row_index + lead, part, 0.0)
        line = part if line is None else line + part
    rows[0, sp] = jnp.sum(line, axis=0, keepdims=True)
    row_copies = []
    for side, step in peers:
        copy = pltpu.make_async_remote_copy(
            src_ref=rows.at[0, sp],
            dst_ref=rows.at[side, sp],
            send_sem=row_send.at[side, step],
            recv_sem=row_recv.at[side, step],
            device_id=peer(side, step),
        )
        copy.start()
        row_copies.append(copy)

    shift_own(pre)

    @pl.loop(1, NX - 1)
    def _(x):
        for h in range(2):
            second_half(("x", x, h))

    receive(pre_copies, pre)

    @pl.loop(0, 2)
    def _(end):
        at = (NX - 1) * end
        for h in range(2):
            second_half(("x", at, h))
        for h in range(2):
            second_half(("y", at, h))

    finish(post_copies)
    finish(cot_copies)
    finish(pre_copies)
    for copy in row_copies:
        copy.wait_recv()
    one_lane = lax.broadcasted_iota(jnp.int32, (1, NZ), 1)
    total = jnp.sum(rows[0], axis=0)
    from_down = jnp.sum(rows[1], axis=0)
    from_up = jnp.sum(rows[2], axis=0)
    total = total + jnp.where(one_lane == 1, pltpu.roll(from_down, NZ - NX, 1), 0.0)
    total = total + jnp.where(one_lane == NX, pltpu.roll(from_up, NX, 1), 0.0)
    total = pltpu.roll(total, NZ - 1, 1) * (1.0 / math.sqrt(spans * NY * NZ))
    profile_ref[...] = total[:, :NX]
    for copy in row_copies:
        copy.wait_send()


def local(flows, spans, populations, gray, fluid_mask, cotangent):
    def vmem(*shape):
        return pltpu.VMEM(shape, jnp.float32)

    zs = len(Z_DIRS)
    faces = [vmem(2, 10, NX, NZ), vmem(2, 10, NX, NZ), vmem(4, 2, 8, NZ)]
    for _ in range(2):
        faces += [vmem(2, 5, NX, NZ), vmem(2, 5, NX, NZ), vmem(4, 1, 8, NZ)]
    adjoint, profile = pl.pallas_call(
        functools.partial(kernel, flows, spans),
        out_shape=(
            jax.ShapeDtypeStruct((19, NX, NY, NZ), jnp.float32),
            jax.ShapeDtypeStruct((1, NX), jnp.float32),
        ),
        in_specs=[pl.BlockSpec(memory_space=pl.ANY)] * 4,
        out_specs=(pl.BlockSpec(memory_space=pltpu.VMEM), pl.BlockSpec(memory_space=pltpu.VMEM)),
        scratch_shapes=[
            vmem(19, NX, NY, NZ),
            vmem(NX, NY, NZ),
            pltpu.VMEM((NX, NY, NZ), jnp.int32),
            vmem(3, NX, NY, NZ),
            vmem(38, NX + 2, PITCH, NZ),
            vmem(2 * zs, NX + 2, PITCH, NZ),
            vmem(19, NX + 2, PITCH, NZ),
            vmem(zs, NX + 2, PITCH, NZ),
            vmem(19, NX + 2, PITCH, NZ),
            vmem(zs, NX + 2, PITCH, NZ),
            *faces,
            vmem(3, NX, 8, NZ),
            vmem(2, 3, NX, NZ),
            vmem(3, spans, 1, NZ),
            pltpu.SemaphoreType.DMA((CHUNKS + 21,)),
            pltpu.SemaphoreType.DMA((3, 8)),
            pltpu.SemaphoreType.DMA((3, 8)),
            pltpu.SemaphoreType.DMA((3, spans)),
            pltpu.SemaphoreType.DMA((3, spans)),
        ],
        compiler_params=pltpu.CompilerParams(
            collective_id=0, has_side_effects=True, vmem_limit_bytes=44 * 1024 * 1024
        ),
    )(*[pltpu.with_memory_space_constraint(x, pltpu.HBM) for x in (populations, gray, fluid_mask, cotangent)])
    return adjoint, profile.reshape(NX)


def solution(mesh):
    placed = (
        P(None, "flow", "span", None),
        P("flow", "span", None),
        P("flow", "span", None),
        P(None, "flow", "span", None),
    )
    return jax.shard_map(
        functools.partial(local, mesh.shape["flow"], mesh.shape["span"]),
        mesh=mesh,
        in_specs=placed,
        out_specs=(P(None, "flow", "span", None), P("flow")),
        check_vma=False,
    )
```

```python
import functools
import math

import jax
import jax.numpy as jnp
from jax import lax
from jax.experimental import pallas as pl
from jax.experimental.pallas import tpu as pltpu
from jax.sharding import PartitionSpec as P

VELOCITY = (
    (0, 0, 0),
    (1, 0, 0), (-1, 0, 0), (0, 1, 0), (0, -1, 0), (0, 0, 1), (0, 0, -1),
    (1, 1, 0), (-1, -1, 0), (1, -1, 0), (-1, 1, 0),
    (1, 0, 1), (-1, 0, -1), (1, 0, -1), (-1, 0, 1),
    (0, 1, 1), (0, -1, -1), (0, 1, -1), (0, -1, 1),
)
ORDER = (1, 7, 9, 11, 13, 2, 8, 10, 12, 14, 0, 3, 4, 5, 6, 15, 16, 17, 18)
SLOT = tuple(ORDER.index(i) for i in range(19))
X_GROUP = {1: 0, -1: 5}
Y_GROUP = {s: tuple(i for i in range(19) if VELOCITY[i][1] == s) for s in (1, -1)}
CORNER = {(1, 1): 7, (-1, -1): 8, (1, -1): 9, (-1, 1): 10}
CORNERS = ((1, 1), (-1, -1), (1, -1), (-1, 1))
PAIRS = ((1, 2), (3, 4), (5, 6), (7, 8), (9, 10), (11, 12), (13, 14), (15, 16), (17, 18))
RATE = 1.0 / 0.6 - 1.2
ENDS = ((0, 1), (0, 2), (1, 2))
Z_DIRS = tuple(i for i in range(19) if VELOCITY[i][2])
PITCH = 32
BASE = 8
NX = 16
NY = 16
NZ = 128
CHUNKS = 4


def split(f):
    even = [f[p] + f[m] for p, m in PAIRS]
    odd = [f[p] - f[m] for p, m in PAIRS]
    return even, odd


def sums(even, odd):
    plane = [even[3 + 2 * k] + even[4 + 2 * k] for k in range(3)]
    cross = [even[3 + 2 * k] - even[4 + 2 * k] for k in range(3)]
    plus = [odd[3 + 2 * k] + odd[4 + 2 * k] for k in range(3)]
    minus = [odd[3 + 2 * k] - odd[4 + 2 * k] for k in range(3)]
    first = [plus[0] + plus[1], minus[0] + plus[2], minus[1] + minus[2]]
    return plane, cross, first


def state_of(f):
    even, odd = split(f)
    plane, cross, first = sums(even, odd)
    j = [odd[a] + first[a] for a in range(3)]
    second = [even[0] + (plane[0] + plane[1]), even[1] + (plane[0] + plane[2]), even[2] + (plane[1] + plane[2])]
    rho = (f[0] + second[0]) + (even[1] + even[2]) + plane[2]
    inv = 1.0 / rho
    u = [entry * inv for entry in j]
    return even, odd, cross, j, second, rho, u


def join(even, odd):
    out = [None] * 19
    for k, (p, m) in enumerate(PAIRS):
        out[p] = even[k] + odd[k]
        out[m] = even[k] - odd[k]
    return out


def collide(f, share, open_voxel):
    even, odd, cross, j, second, rho, u = state_of(f)
    keep = 1.0 - share
    square = [j[a] * u[a] for a in range(3)]
    mixed = [j[0] * u[1], j[0] * u[2], j[1] * u[2]]
    base = rho - 1.5 * (square[0] + square[1] + square[2])
    third = rho * (1.0 / 3.0)
    lack = [second[a] - third - square[a] for a in range(3)]
    rest = 0.4 * base + RATE * (lack[0] + lack[1] + lack[2])
    base_axis = base * (1.0 / 15.0)
    base_edge = base * (1.0 / 30.0)
    grown = [0.15 * square[a] for a in range(3)]
    e_parts = [base_axis + 2.0 * grown[a] - (0.5 * RATE) * lack[a] for a in range(3)]
    o_parts = [0.2 * j[a] for a in range(3)]
    half = [0.1 * j[a] for a in range(3)]
    for k, (a, b) in enumerate(ENDS):
        common = base_edge + (grown[a] + grown[b])
        twist = (5.0 / 12.0) * mixed[k] - (0.25 * RATE) * cross[k]
        e_parts += [common + twist, common - twist]
        o_parts += [half[a] + half[b], half[a] - half[b]]
    drop = join(
        [jnp.where(open_voxel, 0.6 * even[k] - e_parts[k], 0.0) for k in range(9)],
        [jnp.where(open_voxel, -0.4 * odd[k] - o_parts[k], 0.0) for k in range(9)],
    )
    drop[0] = jnp.where(open_voxel, 1.2 * f[0] - rest, 0.0)
    post = [None] * 19
    post[0] = f[0] - keep * drop[0]
    for p, m in PAIRS:
        post[p] = f[m] - keep * drop[p]
        post[m] = f[p] - keep * drop[m]
    return post, drop, u


def pull_back(u, g, share, state=None):
    g_even, g_odd = split(g)
    g_plane, g_cross, g_first = sums(g_even, g_odd)
    keep = 1.0 - share
    k_even = 0.6 * share - 0.1
    k_odd = -0.4 * share - 0.1
    g_axes = g_even[0] + g_even[1] + g_even[2]
    g_edges = g_plane[0] + g_plane[1] + g_plane[2]
    weighted = g[0] * (1.0 / 3.0) + g_axes * (1.0 / 18.0) + g_edges * (1.0 / 36.0)
    both = [g_plane[0] + g_plane[1], g_plane[0] + g_plane[2], g_plane[1] + g_plane[2]]
    diag = [0.5 * g_even[a] - g[0] for a in range(3)]
    side = [0.25 * g_cross[k] for k in range(3)]
    flow = [0.2 * g_odd[a] + 0.1 * g_first[a] for a in range(3)]
    shared = 3.6 * weighted
    entry = [0.6 * g_even[a] + 0.3 * both[a] + (2.0 * RATE) * diag[a] - shared for a in range(3)]
    tilt = [(5.0 / 3.0) * side[k] for k in range(3)]
    turn = [
        u[0] * entry[0] + (tilt[0] * u[1] + tilt[1] * u[2]),
        u[1] * entry[1] + (tilt[0] * u[0] + tilt[2] * u[2]),
        u[2] * entry[2] + (tilt[1] * u[0] + tilt[2] * u[1]),
    ]
    scalar = 1.2 * weighted + (RATE / 3.0) * (diag[0] + diag[1] + diag[2])
    half_turn = [0.5 * turn[a] for a in range(3)]
    bar_rho = scalar - (u[0] * half_turn[0] + u[1] * half_turn[1] + u[2] * half_turn[2])
    grade = None
    if state is not None:
        even, odd, cross, j, second, rho, rest = state
        grade = 1.2 * (g[0] * rest) - rho * scalar
        for a in range(3):
            grade = grade - j[a] * (flow[a] + half_turn[a])
        bend = diag[0] * second[0] + diag[1] * second[1] + diag[2] * second[2]
        bend = bend + (side[0] * cross[0] + side[1] * cross[1] + side[2] * cross[2])
        dot_even = g_even[0] * even[0]
        dot_odd = g_odd[0] * odd[0]
        for k in range(1, 9):
            dot_even = dot_even + g_even[k] * even[k]
            dot_odd = dot_odd + g_odd[k] * odd[k]
        grade = grade + RATE * bend + (0.6 * dot_even - 0.4 * dot_odd)
    bar_rho = keep * bar_rho
    bar_j = [keep * (flow[a] + turn[a]) for a in range(3)]
    scale = keep * RATE
    diag = [scale * entry_a for entry_a in diag]
    side = [scale * entry_k for entry_k in side]
    e_parts = [bar_rho - diag[a] for a in range(3)]
    o_parts = list(bar_j)
    for k, (a, b) in enumerate(ENDS):
        common = e_parts[a] - diag[b]
        e_parts += [common - side[k], common + side[k]]
        o_parts += [bar_j[a] + bar_j[b], bar_j[a] - bar_j[b]]
    out = join(
        [k_even * g_even[k] + e_parts[k] for k in range(9)],
        [k_odd * g_odd[k] + o_parts[k] for k in range(9)],
    )
    out[0] = 2.0 * (k_even * g[0]) + bar_rho
    return out, grade


def lane_shift(value, step, lane):
    if step == 0:
        return value
    if step > 0:
        return jnp.where(lane == 0, 0.0, pltpu.roll(value, 1, 1))
    return jnp.where(lane == NZ - 1, 0.0, pltpu.roll(value, NZ - 1, 1))


class Field:
    def __init__(self, raw, shifted, y_send, y_recv, c_recv, sign, sends, recvs):
        self.raw, self.shifted = raw, shifted
        self.flat_raw = raw.reshape(19, (NX + 2) * PITCH, NZ)
        self.flat_shifted = shifted.reshape(len(Z_DIRS), (NX + 2) * PITCH, NZ)
        self.y_send, self.y_recv, self.c_recv = y_send, y_recv, c_recv
        self.sign, self.sends, self.recvs = sign, sends, recvs

    def pick(self, i):
        if VELOCITY[i][2]:
            return self.shifted, self.flat_shifted, Z_DIRS.index(i)
        return self.raw, self.flat_raw, SLOT[i]


def kernel(
    flows, spans,
    pop_hbm, gray_hbm, mask_hbm, cot_hbm,
    out_ref, profile_ref,
    pop, gray, mask, speed,
    post_raw, post_z, drop_raw, drop_z, cot_raw, cot_z, pre_raw, pre_z,
    post_ys, post_yr, post_cr, drop_ys, drop_yr, drop_cr, cot_ys, cot_yr, cot_cr, pre_ys, pre_yr, pre_cr,
    grades, y_grades, rows,
    in_sems, far_sems, send_sems, recv_sems, row_send, row_recv,
):
    fl = lax.axis_index("flow")
    sp = lax.axis_index("span")
    up = lax.rem(fl + 1, flows)
    down = lax.rem(fl + flows - 1, flows)
    flow_at = {1: up, -1: down}
    span_at = {1: sp + 1, -1: sp - 1}
    inside = {1: sp < spans - 1, -1: sp > 0}
    post = Field(post_raw, post_z, post_ys, post_yr, post_cr, 1, send_sems.at[0], recv_sems.at[0])
    cot = Field(cot_raw, cot_z, cot_ys, cot_yr, cot_cr, -1, send_sems.at[1], recv_sems.at[1])
    pre = Field(pre_raw, pre_z, pre_ys, pre_yr, pre_cr, -1, send_sems.at[2], recv_sems.at[2])
    drop = Field(drop_raw, drop_z, drop_ys, drop_yr, drop_cr, 1, send_sems.at[3], recv_sems.at[3])

    def target(step_x, step_y):
        return {
            "flow": flow_at[step_x] if step_x else fl,
            "span": span_at[step_y] if step_y else sp,
        }

    chunk = NX // CHUNKS
    pop_loads = [
        pltpu.make_async_copy(
            pop_hbm.at[:, pl.ds(chunk * c, chunk)], pop.at[:, pl.ds(chunk * c, chunk)], in_sems.at[c]
        )
        for c in range(CHUNKS)
    ]
    side_loads = [
        pltpu.make_async_copy(gray_hbm, gray, in_sems.at[CHUNKS]),
        pltpu.make_async_copy(mask_hbm, mask, in_sems.at[CHUNKS + 1]),
    ]
    cot_loads = [
        pltpu.make_async_copy(
            cot_hbm.at[ORDER[k]], cot_raw.at[k, pl.ds(1, NX), pl.ds(BASE, NY), :], in_sems.at[CHUNKS + 2 + k]
        )
        for k in range(19)
    ]
    pop_loads[0].start()
    for load in side_loads + pop_loads[1:] + cot_loads:
        load.start()

    steps = sorted(range(spans), key=lambda d: -min(d, spans - d))
    peers = [(side, step) for step in steps for side in (0, 1, 2) if side or step]

    def peer(side, step):
        return {"flow": (fl, up, down)[side], "span": lax.rem(sp + step, spans) if step else sp}

    barrier = pltpu.get_barrier_semaphore()
    for step_x in (1, -1):
        pl.semaphore_signal(barrier, inc=1, device_id=target(step_x, 0))
    for step_y in (1, -1):

        @pl.when(inside[step_y])
        def _():
            for step_x in (1, -1, 0):
                pl.semaphore_signal(barrier, inc=1, device_id=target(step_x, step_y))

    def count_at(distance):
        return (sp >= distance).astype(jnp.int32) + (sp + distance < spans).astype(jnp.int32)

    def greet(semaphore, distance):
        @pl.when(sp >= distance)
        def _():
            pl.semaphore_signal(semaphore, inc=1, device_id={"flow": fl, "span": sp - distance})

        @pl.when(sp + distance < spans)
        def _():
            pl.semaphore_signal(semaphore, inc=1, device_id={"flow": fl, "span": sp + distance})

    greet(barrier, 2)

    distances = []
    while 2 << len(distances) < spans:
        distances.append(2 << len(distances))

    def hear(stage):
        if stage < len(distances):
            pl.semaphore_wait(far_sems.at[stage], count_at(distances[stage]))

    def tell(stage):
        if stage < len(distances):
            greet(far_sems.at[stage], distances[stage])

    def copies(field):
        buf, sign = field.raw, field.sign
        made = []

        def remote(src, dst, index, where, sent, received):
            copy = pltpu.make_async_remote_copy(
                src_ref=src,
                dst_ref=dst,
                send_sem=field.sends.at[index],
                recv_sem=field.recvs.at[index],
                device_id=where,
            )
            made.append((copy, sent, received))

        for n, (step_x, step_y) in enumerate(CORNERS):
            slot = SLOT[CORNER[(sign * step_x, sign * step_y)]]
            plane = NX if step_x > 0 else 1
            row = BASE + (NY - 8 if step_y > 0 else 0)
            src = buf.at[slot, plane, pl.ds(row, 8), :]
            remote(src, field.c_recv.at[n], 4 + n, target(step_x, step_y), inside[step_y], inside[-step_y])
        for n, step in enumerate((1, -1)):
            remote(field.y_send.at[n], field.y_recv.at[n], 2 + n, target(0, step), inside[step], inside[-step])
        for n, step in enumerate((1, -1)):
            group = pl.ds(X_GROUP[sign * step], 5)
            src = buf.at[group, NX if step > 0 else 1, pl.ds(BASE, NY), :]
            dst = buf.at[group, 0 if step > 0 else NX + 1, pl.ds(BASE, NY), :]
            remote(src, dst, n, target(step, 0), None, None)
        return made

    def pack(field):
        for n, step in enumerate((1, -1)):
            row = PITCH + BASE + (NY - 1 if step > 0 else 0)
            for k, i in enumerate(Y_GROUP[field.sign * step]):
                field.y_send[n, k] = field.flat_raw[SLOT[i], pl.ds(row, NX, stride=PITCH), :]

    def send(*fields):
        made = [copies(field) for field in fields]
        for several in zip(*made):
            for copy, sent, _ in several:
                if sent is None:
                    copy.start()
                else:
                    pl.when(sent)(copy.start)
        return made

    lane = lax.broadcasted_iota(jnp.int32, (8, NZ), 1)
    wide_lane = lax.broadcasted_iota(jnp.int32, (NX, NZ), 1)
    row_at = lax.broadcasted_iota(jnp.int32, (8, NZ), 0)

    def receive(made, field):
        sign = field.sign
        for copy, _, received in made:
            if received is None:
                copy.wait_recv()
            else:
                pl.when(received)(copy.wait_recv)
        for n, step in enumerate((1, -1)):
            row = PITCH + BASE + (-1 if step > 0 else NY)

            def place(step=step, n=n, row=row, empty=False):
                for k, i in enumerate(Y_GROUP[sign * step]):
                    _, flat, slot = field.pick(i)
                    if empty:
                        value = jnp.zeros((NX, NZ), jnp.float32)
                    else:
                        value = lane_shift(field.y_recv[n, k], sign * VELOCITY[i][2], wide_lane)
                    flat[slot, pl.ds(row, NX, stride=PITCH), :] = value
                for m, (step_x, step_y) in enumerate(CORNERS):
                    if step_y != step:
                        continue
                    i = CORNER[(sign * step_x, sign * step_y)]
                    at = 7 if step_y > 0 else 0
                    plane = 0 if step_x > 0 else NX + 1
                    corner = jnp.zeros((1, NZ), jnp.float32) if empty else field.c_recv[m, pl.ds(at, 1), :]
                    field.raw[SLOT[i], plane, pl.ds(BASE + (-1 if step > 0 else NY), 1), :] = corner

            pl.when(inside[-step])(place)
            pl.when(jnp.logical_not(inside[-step]))(functools.partial(place, empty=True))
        for plane, step in ((0, 1), (NX + 1, -1)):
            for i in Z_DIRS:
                if VELOCITY[i][0] != sign * step:
                    continue
                for h in range(2):
                    field.shifted[Z_DIRS.index(i), plane, pl.ds(BASE + 8 * h, 8), :] = lane_shift(
                        field.raw[SLOT[i], plane, pl.ds(BASE + 8 * h, 8), :], sign * VELOCITY[i][2], lane
                    )

    def finish(made):
        for copy, sent, _ in made:
            if sent is None:
                copy.wait_send()
            else:
                pl.when(sent)(copy.wait_send)

    def shift_own(field):
        @pl.loop(0, NX // 4)
        def _(block):
            values = []
            for i in Z_DIRS:
                for q in range(4):
                    for h in range(2):
                        at = (4 * block + q + 1, pl.ds(BASE + 8 * h, 8))
                        value = field.raw[SLOT[i], at[0], at[1], :]
                        values.append((i, at, lane_shift(value, field.sign * VELOCITY[i][2], lane)))
            for i, at, value in values:
                field.shifted[Z_DIRS.index(i), at[0], at[1], :] = value

    def moved(field, tile, which=range(19)):
        kind, at, h = tile
        values = []
        for i in which:
            step_x, step_y = field.sign * VELOCITY[i][0], field.sign * VELOCITY[i][1]
            ref, flat, slot = field.pick(i)
            if kind == "x":
                values.append(ref[slot, at + 1 - step_x, pl.ds(BASE + 8 * h - step_y, 8), :])
            else:
                start = (8 * h + 1 - step_x) * PITCH + BASE - step_y + at
                values.append(flat[slot, pl.ds(start, 8, stride=PITCH), :])
        return values

    def flat_of(ref):
        shape = ref.shape
        return ref.reshape(*shape[:-3], NX * NY, NZ)

    def own(ref, tile, *lead):
        kind, at, h = tile
        if kind == "x":
            return ref[(*lead, at, pl.ds(8 * h, 8), slice(None))]
        return flat_of(ref)[(*lead, pl.ds(8 * NY * h + at, 8, stride=NY), slice(None))]

    def share_of(tile):
        open_voxel = own(mask, tile) == 1
        return jnp.where(open_voxel, own(gray, tile), 1.0), open_voxel

    def products(parts, values, tile, which):
        for i, value in zip(which, moved(drop, tile, which)):
            index = (0, 1, 2)[VELOCITY[i][0]]
            term = values[i] * value
            parts[index] = term if parts[index] is None else parts[index] + term

    def late(tile):
        kind, at, h = tile
        at_end, at_half = (1 if at == 0 else -1), (1 if h == 0 else -1)
        steps = (at_end, at_half) if kind == "x" else (at_half, at_end)
        return [i for i in range(19) if VELOCITY[i][0] == steps[0] or VELOCITY[i][1] == steps[1]]

    def first_half(tile, left=()):
        kind, at, h = tile
        f = moved(post, tile)
        even, odd, cross, j, second, rho, u = state_of(f)
        share, open_voxel = share_of(tile)
        out, grade = pull_back(u, moved(cot, tile), share, (even, odd, cross, j, second, rho, f[0]))
        centre = jnp.where(open_voxel, grade, 0.0)
        parts = [centre, None, None]
        products(parts, out, tile, [i for i in range(19) if i not in left])
        for i in range(19):
            if kind == "x":
                pre_raw[SLOT[i], at + 1, pl.ds(BASE + 8 * h, 8), :] = out[i]
            else:
                start = (8 * h + 1) * PITCH + BASE + at
                pre.flat_raw[SLOT[i], pl.ds(start, 8, stride=PITCH), :] = out[i]
        return parts

    def rest_of(tile):
        kind, at, h = tile
        which = late(tile)
        values = {}
        for i in which:
            if kind == "x":
                values[i] = pre_raw[SLOT[i], at + 1, pl.ds(BASE + 8 * h, 8), :]
            else:
                start = (8 * h + 1) * PITCH + BASE + at
                values[i] = pre.flat_raw[SLOT[i], pl.ds(start, 8, stride=PITCH), :]
        parts = [None, None, None]
        products(parts, values, tile, which)
        return parts

    def second_half(tile):
        kind, at, h = tile
        share, _ = share_of(tile)
        out, _ = pull_back([own(speed, tile, a) for a in range(3)], moved(pre, tile), share)
        for i in range(19):
            if kind == "x":
                out_ref[i, at, pl.ds(8 * h, 8), :] = out[i]
            else:
                flat_of(out_ref)[i, pl.ds(8 * NY * h + at, 8, stride=NY), :] = out[i]

    def without_edge(h, value):
        return jnp.where(row_at == 7 * h, 0.0, value)

    for load in side_loads:
        load.wait()

    def first_collision(x):
        for h in range(2):
            tile = ("x", x, h)
            share, open_voxel = share_of(tile)
            made, lost, u = collide([own(pop, tile, i) for i in range(19)], share, open_voxel)
            for i in range(19):
                post_raw[SLOT[i], x + 1, pl.ds(BASE + 8 * h, 8), :] = made[i]
                drop_raw[SLOT[i], x + 1, pl.ds(BASE + 8 * h, 8), :] = lost[i]
            for a in range(3):
                speed[a, x, pl.ds(8 * h, 8), :] = u[a]

    for c in range(CHUNKS):
        pop_loads[c].wait()

        @pl.loop(chunk * c, chunk * (c + 1))
        def _(x):
            first_collision(x)

    pack(post)
    for load in cot_loads:
        load.wait()
    pack(cot)
    pl.semaphore_wait(barrier, 2 + 3 * count_at(1) + count_at(2))
    post_copies, cot_copies = send(post, cot)
    tell(0)
    pack(drop)
    (drop_copies,) = send(drop)
    shift_own(post)
    shift_own(cot)
    hear(0)
    tell(1)
    shift_own(drop)

    @pl.loop(1, NX - 1)
    def _(x):
        halves = [[without_edge(h, part) for part in first_half(("x", x, h))] for h in range(2)]
        for q in range(3):
            grades[q, x] = halves[0][q] + halves[1][q]

    hear(1)
    tell(2)
    receive(cot_copies, cot)
    receive(post_copies, post)

    for end in (0, 1):
        at = (NX - 1) * end
        halves = [first_half(("x", at, h), late(("x", at, h))) for h in range(2)]
        for q in range(3):
            both = [part[q] for part in halves if part[q] is not None]
            grades[q, at] = functools.reduce(jnp.add, both) if both else jnp.zeros((8, NZ), jnp.float32)
        for h in range(2):
            for q, part in enumerate(first_half(("y", at, h), late(("y", at, h)))):
                kept = jnp.zeros((8, NZ), jnp.float32) if part is None else without_edge(h, part)
                y_grades[end, q, pl.ds(8 * h, 8), :] = kept

    pack(pre)
    (pre_copies,) = send(pre)
    receive(drop_copies, drop)
    for end in (0, 1):
        at = (NX - 1) * end
        shares = [rest_of(("x", at, h)) for h in range(2)]
        for q in range(3):
            both = [part[q] for part in shares if part[q] is not None]
            if both:
                grades[q, at] += functools.reduce(jnp.add, both)
        for h in range(2):
            for q, part in enumerate(rest_of(("y", at, h))):
                if part is not None:
                    y_grades[end, q, pl.ds(8 * h, 8), :] += without_edge(h, part)

    line = None
    row_index = lax.broadcasted_iota(jnp.int32, (NX, NZ), 0)
    for q, lead in enumerate((1, 0, 2)):
        part = jnp.sum(grades[q], axis=1) + (y_grades[0, q] + y_grades[1, q])
        part = jnp.sum(part, axis=1, keepdims=True)
        part = jnp.where(wide_lane == row_index + lead, part, 0.0)
        line = part if line is None else line + part
    rows[0, sp] = jnp.sum(line, axis=0, keepdims=True)
    hear(2)
    row_copies = []
    for side, step in peers:
        copy = pltpu.make_async_remote_copy(
            src_ref=rows.at[0, sp],
            dst_ref=rows.at[side, sp],
            send_sem=row_send.at[side, step],
            recv_sem=row_recv.at[side, step],
            device_id=peer(side, step),
        )
        copy.start()
        row_copies.append(copy)

    shift_own(pre)

    @pl.loop(1, NX - 1)
    def _(x):
        for h in range(2):
            second_half(("x", x, h))

    receive(pre_copies, pre)

    @pl.loop(0, 2)
    def _(end):
        at = (NX - 1) * end
        for h in range(2):
            second_half(("x", at, h))
        for h in range(2):
            second_half(("y", at, h))

    finish(post_copies)
    finish(drop_copies)
    finish(cot_copies)
    finish(pre_copies)
    for copy in row_copies:
        copy.wait_recv()
    one_lane = lax.broadcasted_iota(jnp.int32, (1, NZ), 1)
    total = jnp.sum(rows[0], axis=0)
    from_down = jnp.sum(rows[1], axis=0)
    from_up = jnp.sum(rows[2], axis=0)
    total = total + jnp.where(one_lane == 1, pltpu.roll(from_down, NZ - NX, 1), 0.0)
    total = total + jnp.where(one_lane == NX, pltpu.roll(from_up, NX, 1), 0.0)
    total = pltpu.roll(total, NZ - 1, 1) * (1.0 / math.sqrt(spans * NY * NZ))
    profile_ref[...] = total[:, :NX]
    for copy in row_copies:
        copy.wait_send()


def local(flows, spans, populations, gray, fluid_mask, cotangent):
    def vmem(*shape):
        return pltpu.VMEM(shape, jnp.float32)

    zs = len(Z_DIRS)
    faces = [vmem(2, 5, NX, NZ), vmem(2, 5, NX, NZ), vmem(4, 8, NZ)] * 4
    adjoint, profile = pl.pallas_call(
        functools.partial(kernel, flows, spans),
        out_shape=(
            jax.ShapeDtypeStruct((19, NX, NY, NZ), jnp.float32),
            jax.ShapeDtypeStruct((1, NX), jnp.float32),
        ),
        in_specs=[pl.BlockSpec(memory_space=pl.ANY)] * 4,
        out_specs=(pl.BlockSpec(memory_space=pltpu.VMEM), pl.BlockSpec(memory_space=pltpu.VMEM)),
        scratch_shapes=[
            vmem(19, NX, NY, NZ),
            vmem(NX, NY, NZ),
            pltpu.VMEM((NX, NY, NZ), jnp.int32),
            vmem(3, NX, NY, NZ),
            *[vmem(19, NX + 2, PITCH, NZ), vmem(zs, NX + 2, PITCH, NZ)] * 4,
            *faces,
            vmem(3, NX, 8, NZ),
            vmem(2, 3, NX, NZ),
            vmem(3, spans, 1, NZ),
            pltpu.SemaphoreType.DMA((CHUNKS + 21,)),
            pltpu.SemaphoreType.REGULAR((4,)),
            pltpu.SemaphoreType.DMA((4, 8)),
            pltpu.SemaphoreType.DMA((4, 8)),
            pltpu.SemaphoreType.DMA((3, spans)),
            pltpu.SemaphoreType.DMA((3, spans)),
        ],
        compiler_params=pltpu.CompilerParams(
            collective_id=0, has_side_effects=True, vmem_limit_bytes=44 * 1024 * 1024
        ),
    )(*[pltpu.with_memory_space_constraint(x, pltpu.HBM) for x in (populations, gray, fluid_mask, cotangent)])
    return adjoint, profile.reshape(NX)


def solution(mesh):
    placed = (
        P(None, "flow", "span", None),
        P("flow", "span", None),
        P("flow", "span", None),
        P(None, "flow", "span", None),
    )
    return jax.shard_map(
        functools.partial(local, mesh.shape["flow"], mesh.shape["span"]),
        mesh=mesh,
        in_specs=placed,
        out_specs=(P(None, "flow", "span", None), P("flow")),
        check_vma=False,
    )
```

```python
import functools
import math

import jax
import jax.numpy as jnp
from jax import lax
from jax.experimental import pallas as pl
from jax.experimental.pallas import tpu as pltpu
from jax.sharding import PartitionSpec as P

VELOCITY = (
    (0, 0, 0),
    (1, 0, 0), (-1, 0, 0), (0, 1, 0), (0, -1, 0), (0, 0, 1), (0, 0, -1),
    (1, 1, 0), (-1, -1, 0), (1, -1, 0), (-1, 1, 0),
    (1, 0, 1), (-1, 0, -1), (1, 0, -1), (-1, 0, 1),
    (0, 1, 1), (0, -1, -1), (0, 1, -1), (0, -1, 1),
)
ORDER = (1, 7, 9, 11, 13, 2, 8, 10, 12, 14, 0, 3, 4, 5, 6, 15, 16, 17, 18)
SLOT = tuple(ORDER.index(i) for i in range(19))
X_GROUP = {1: 0, -1: 5}
Y_GROUP = {s: tuple(i for i in range(19) if VELOCITY[i][1] == s) for s in (1, -1)}
CORNER = {(1, 1): 7, (-1, -1): 8, (1, -1): 9, (-1, 1): 10}
PAIRS = ((1, 2), (3, 4), (5, 6), (7, 8), (9, 10), (11, 12), (13, 14), (15, 16), (17, 18))
RATE = 1.0 / 0.6 - 1.2
ENDS = ((0, 1), (0, 2), (1, 2))
Z_DIRS = tuple(i for i in range(19) if VELOCITY[i][2])
PITCH = 32
BASE = 8
NX = 16
NY = 16
NZ = 128
CHUNKS = 2


def split(f):
    even = [f[p] + f[m] for p, m in PAIRS]
    odd = [f[p] - f[m] for p, m in PAIRS]
    return even, odd


def sums(even, odd):
    plane = [even[3 + 2 * k] + even[4 + 2 * k] for k in range(3)]
    cross = [even[3 + 2 * k] - even[4 + 2 * k] for k in range(3)]
    plus = [odd[3 + 2 * k] + odd[4 + 2 * k] for k in range(3)]
    minus = [odd[3 + 2 * k] - odd[4 + 2 * k] for k in range(3)]
    first = [plus[0] + plus[1], minus[0] + plus[2], minus[1] + minus[2]]
    return plane, cross, first


def state_of(f):
    even, odd = split(f)
    plane, cross, first = sums(even, odd)
    j = [odd[a] + first[a] for a in range(3)]
    second = [even[0] + (plane[0] + plane[1]), even[1] + (plane[0] + plane[2]), even[2] + (plane[1] + plane[2])]
    rho = (f[0] + second[0]) + (even[1] + even[2]) + plane[2]
    inv = 1.0 / rho
    u = [entry * inv for entry in j]
    return even, odd, cross, j, second, rho, u


def join(even, odd):
    out = [None] * 19
    for k, (p, m) in enumerate(PAIRS):
        out[p] = even[k] + odd[k]
        out[m] = even[k] - odd[k]
    return out


def collide(f, share, open_voxel):
    even, odd, cross, j, second, rho, u = state_of(f)
    keep = 1.0 - share
    square = [j[a] * u[a] for a in range(3)]
    mixed = [j[0] * u[1], j[0] * u[2], j[1] * u[2]]
    base = rho - 1.5 * (square[0] + square[1] + square[2])
    third = rho * (1.0 / 3.0)
    lack = [second[a] - third - square[a] for a in range(3)]
    rest = 0.4 * base + RATE * (lack[0] + lack[1] + lack[2])
    base_axis = base * (1.0 / 15.0)
    base_edge = base * (1.0 / 30.0)
    grown = [0.15 * square[a] for a in range(3)]
    e_parts = [base_axis + 2.0 * grown[a] - (0.5 * RATE) * lack[a] for a in range(3)]
    o_parts = [0.2 * j[a] for a in range(3)]
    half = [0.1 * j[a] for a in range(3)]
    for k, (a, b) in enumerate(ENDS):
        common = base_edge + (grown[a] + grown[b])
        twist = (5.0 / 12.0) * mixed[k] - (0.25 * RATE) * cross[k]
        e_parts += [common + twist, common - twist]
        o_parts += [half[a] + half[b], half[a] - half[b]]
    drop = join(
        [jnp.where(open_voxel, 0.6 * even[k] - e_parts[k], 0.0) for k in range(9)],
        [jnp.where(open_voxel, -0.4 * odd[k] - o_parts[k], 0.0) for k in range(9)],
    )
    drop[0] = jnp.where(open_voxel, 1.2 * f[0] - rest, 0.0)
    post = [None] * 19
    post[0] = f[0] - keep * drop[0]
    for p, m in PAIRS:
        post[p] = f[m] - keep * drop[p]
        post[m] = f[p] - keep * drop[m]
    return post, drop, u


def pull_back(u, g, share, state=None):
    g_even, g_odd = split(g)
    g_plane, g_cross, g_first = sums(g_even, g_odd)
    keep = 1.0 - share
    k_even = 0.6 * share - 0.1
    k_odd = -0.4 * share - 0.1
    g_axes = g_even[0] + g_even[1] + g_even[2]
    g_edges = g_plane[0] + g_plane[1] + g_plane[2]
    weighted = g[0] * (1.0 / 3.0) + g_axes * (1.0 / 18.0) + g_edges * (1.0 / 36.0)
    both = [g_plane[0] + g_plane[1], g_plane[0] + g_plane[2], g_plane[1] + g_plane[2]]
    diag = [0.5 * g_even[a] - g[0] for a in range(3)]
    side = [0.25 * g_cross[k] for k in range(3)]
    flow = [0.2 * g_odd[a] + 0.1 * g_first[a] for a in range(3)]
    shared = 3.6 * weighted
    entry = [0.6 * g_even[a] + 0.3 * both[a] + (2.0 * RATE) * diag[a] - shared for a in range(3)]
    tilt = [(5.0 / 3.0) * side[k] for k in range(3)]
    turn = [
        u[0] * entry[0] + (tilt[0] * u[1] + tilt[1] * u[2]),
        u[1] * entry[1] + (tilt[0] * u[0] + tilt[2] * u[2]),
        u[2] * entry[2] + (tilt[1] * u[0] + tilt[2] * u[1]),
    ]
    scalar = 1.2 * weighted + (RATE / 3.0) * (diag[0] + diag[1] + diag[2])
    half_turn = [0.5 * turn[a] for a in range(3)]
    bar_rho = scalar - (u[0] * half_turn[0] + u[1] * half_turn[1] + u[2] * half_turn[2])
    grade = None
    if state is not None:
        even, odd, cross, j, second, rho, rest = state
        grade = 1.2 * (g[0] * rest) - rho * scalar
        for a in range(3):
            grade = grade - j[a] * (flow[a] + half_turn[a])
        bend = diag[0] * second[0] + diag[1] * second[1] + diag[2] * second[2]
        bend = bend + (side[0] * cross[0] + side[1] * cross[1] + side[2] * cross[2])
        dot_even = g_even[0] * even[0]
        dot_odd = g_odd[0] * odd[0]
        for k in range(1, 9):
            dot_even = dot_even + g_even[k] * even[k]
            dot_odd = dot_odd + g_odd[k] * odd[k]
        grade = grade + RATE * bend + (0.6 * dot_even - 0.4 * dot_odd)
    bar_rho = keep * bar_rho
    bar_j = [keep * (flow[a] + turn[a]) for a in range(3)]
    scale = keep * RATE
    diag = [scale * entry_a for entry_a in diag]
    side = [scale * entry_k for entry_k in side]
    e_parts = [bar_rho - diag[a] for a in range(3)]
    o_parts = list(bar_j)
    for k, (a, b) in enumerate(ENDS):
        common = e_parts[a] - diag[b]
        e_parts += [common - side[k], common + side[k]]
        o_parts += [bar_j[a] + bar_j[b], bar_j[a] - bar_j[b]]
    out = join(
        [k_even * g_even[k] + e_parts[k] for k in range(9)],
        [k_odd * g_odd[k] + o_parts[k] for k in range(9)],
    )
    out[0] = 2.0 * (k_even * g[0]) + bar_rho
    return out, grade


def lane_shift(value, step, lane):
    if step == 0:
        return value
    if step > 0:
        return jnp.where(lane == 0, 0.0, pltpu.roll(value, 1, 1))
    return jnp.where(lane == NZ - 1, 0.0, pltpu.roll(value, NZ - 1, 1))


class Field:
    def __init__(self, index, raw, shifted, y_send, y_recv, sign, recvs):
        self.index, self.raw, self.shifted = index, raw, shifted
        self.flat_raw = raw.reshape(19, (NX + 2) * PITCH, NZ)
        self.flat_shifted = shifted.reshape(len(Z_DIRS), (NX + 2) * PITCH, NZ)
        self.y_send, self.y_recv = y_send, y_recv
        self.sign, self.recvs = sign, recvs

    def pick(self, i):
        if VELOCITY[i][2]:
            return self.shifted, self.flat_shifted, Z_DIRS.index(i)
        return self.raw, self.flat_raw, SLOT[i]


def kernel(
    flows, spans,
    pop_hbm, gray_hbm, mask_hbm, cot_hbm,
    out_ref, profile_ref,
    pop, gray, mask, speed,
    post_raw, post_z, drop_raw, drop_z, cot_raw, cot_z, pre_raw, pre_z,
    y_send, y_recv, grades, y_grades, line_ref, rows,
    in_sems, far_sems, send_sems, recv_sems, row_sems,
):
    fl = lax.axis_index("flow")
    sp = lax.axis_index("span")
    up = lax.rem(fl + 1, flows)
    down = lax.rem(fl + flows - 1, flows)
    flow_at = {1: up, -1: down}
    span_at = {1: sp + 1, -1: sp - 1}
    inside = {1: sp < spans - 1, -1: sp > 0}
    post = Field(0, post_raw, post_z, y_send.at[0], y_recv.at[0], 1, recv_sems.at[0])
    cot = Field(1, cot_raw, cot_z, y_send.at[1], y_recv.at[1], -1, recv_sems.at[0])
    drop = Field(2, drop_raw, drop_z, y_send.at[2], y_recv.at[2], 1, recv_sems.at[1])
    pre = Field(3, pre_raw, pre_z, y_send.at[3], y_recv.at[3], -1, recv_sems.at[2])

    def target(step_x, step_y):
        return {
            "flow": flow_at[step_x] if step_x else fl,
            "span": span_at[step_y] if step_y else sp,
        }

    chunk = NX // CHUNKS
    pop_loads = [
        pltpu.make_async_copy(
            pop_hbm.at[:, pl.ds(chunk * c, chunk)], pop.at[:, pl.ds(chunk * c, chunk)], in_sems.at[c]
        )
        for c in range(CHUNKS)
    ]
    side_loads = [
        pltpu.make_async_copy(gray_hbm, gray, in_sems.at[CHUNKS]),
        pltpu.make_async_copy(mask_hbm, mask, in_sems.at[CHUNKS + 1]),
    ]
    cot_loads = [
        pltpu.make_async_copy(
            cot_hbm.at[ORDER[k]], cot_raw.at[k, pl.ds(1, NX), pl.ds(BASE, NY), :], in_sems.at[CHUNKS + 2]
        )
        for k in range(19)
    ]
    pop_loads[0].start()
    for load in side_loads + pop_loads[1:] + cot_loads:
        load.start()

    def take(ref, semaphore):
        pltpu.make_async_copy(ref, ref, semaphore).wait()

    steps = sorted(range(spans), key=lambda d: -min(d, spans - d))
    peers = [(side, step) for step in steps for side in (0, 1, 2) if side or step]

    def peer(side, step):
        return {"flow": (fl, up, down)[side], "span": lax.rem(sp + step, spans) if step else sp}

    barrier = pltpu.get_barrier_semaphore()
    for step_x in (1, -1):
        pl.semaphore_signal(barrier, inc=1, device_id=target(step_x, 0))
    for step_y in (1, -1):

        @pl.when(inside[step_y])
        def _():
            for step_x in (1, -1, 0):
                pl.semaphore_signal(barrier, inc=1, device_id=target(step_x, step_y))

    def count_at(distance):
        return (sp >= distance).astype(jnp.int32) + (sp + distance < spans).astype(jnp.int32)

    def greet(semaphore, distance):
        @pl.when(sp >= distance)
        def _():
            pl.semaphore_signal(semaphore, inc=1, device_id={"flow": fl, "span": sp - distance})

        @pl.when(sp + distance < spans)
        def _():
            pl.semaphore_signal(semaphore, inc=1, device_id={"flow": fl, "span": sp + distance})

    greet(barrier, 2)

    distances = []
    while 2 << len(distances) < spans:
        distances.append(2 << len(distances))

    def hear(stage):
        if stage < len(distances):
            pl.semaphore_wait(far_sems.at[stage], count_at(distances[stage]))

    def tell(stage):
        if stage < len(distances):
            greet(far_sems.at[stage], distances[stage])

    def copies(field):
        buf, sign = field.raw, field.sign
        across, along = [], []

        def remote(src, dst, index, where):
            return pltpu.make_async_remote_copy(
                src_ref=src,
                dst_ref=dst,
                send_sem=send_sems.at[index],
                recv_sem=field.recvs.at[index],
                device_id=where,
            )

        for n, step in enumerate((1, -1)):
            for m, step_x in enumerate((1, -1)):
                slot = SLOT[CORNER[(sign * step_x, sign * step)]]
                plane = NX if step_x > 0 else 1
                src = buf.at[slot, plane, pl.ds(BASE + (NY - 8 if step > 0 else 0), 8), :]
                dst = field.y_recv.at[n, 5, pl.ds(8 * m, 8), :]
                across.append((remote(src, dst, n, target(step_x, step)), inside[step]))
        for n, step in enumerate((1, -1)):
            src, dst = field.y_send.at[n], field.y_recv.at[n, pl.ds(0, 5)]
            across.append((remote(src, dst, n, target(0, step)), inside[step]))
        for n, step in enumerate((1, -1)):
            group = pl.ds(X_GROUP[sign * step], 5)
            src = buf.at[group, NX if step > 0 else 1, pl.ds(BASE, NY), :]
            dst = buf.at[group, 0 if step > 0 else NX + 1, pl.ds(BASE, NY), :]
            along.append((remote(src, dst, 2, target(step, 0)), None))
        return across, along

    def pack(field):
        for n, step in enumerate((1, -1)):
            row = PITCH + BASE + (NY - 1 if step > 0 else 0)
            for k, i in enumerate(Y_GROUP[field.sign * step]):
                field.y_send[n, k] = field.flat_raw[SLOT[i], pl.ds(row, NX, stride=PITCH), :]

    def send(*made):
        for copy, sent in made:
            if sent is None:
                copy.start()
            else:
                pl.when(sent)(copy.start)

    lane = lax.broadcasted_iota(jnp.int32, (8, NZ), 1)
    wide_lane = lax.broadcasted_iota(jnp.int32, (NX, NZ), 1)
    row_at = lax.broadcasted_iota(jnp.int32, (8, NZ), 0)

    def arrive(*fields):
        first, recvs = fields[0], fields[0].recvs
        for n, step in enumerate((1, -1)):
            came = y_recv.at[pl.ds(first.index, len(fields)), n]
            pl.when(inside[-step])(functools.partial(take, came, recvs.at[n]))
        take(first.raw.at[pl.ds(0, 10), pl.ds(0, len(fields)), pl.ds(BASE, NY), :], recvs.at[2])

    def receive(field):
        sign = field.sign
        for n, step in enumerate((1, -1)):
            row = PITCH + BASE + (-1 if step > 0 else NY)

            def place(step=step, n=n, row=row, empty=False):
                for k, i in enumerate(Y_GROUP[sign * step]):
                    _, flat, slot = field.pick(i)
                    if empty:
                        value = jnp.zeros((NX, NZ), jnp.float32)
                    else:
                        value = lane_shift(field.y_recv[n, k], sign * VELOCITY[i][2], wide_lane)
                    flat[slot, pl.ds(row, NX, stride=PITCH), :] = value
                for m, step_x in enumerate((1, -1)):
                    i = CORNER[(sign * step_x, sign * step)]
                    at = 8 * m + (7 if step > 0 else 0)
                    plane = 0 if step_x > 0 else NX + 1
                    corner = jnp.zeros((1, NZ), jnp.float32) if empty else field.y_recv[n, 5, pl.ds(at, 1), :]
                    field.raw[SLOT[i], plane, pl.ds(BASE + (-1 if step > 0 else NY), 1), :] = corner

            pl.when(inside[-step])(place)
            pl.when(jnp.logical_not(inside[-step]))(functools.partial(place, empty=True))
        for plane, step in ((0, 1), (NX + 1, -1)):
            for i in Z_DIRS:
                if VELOCITY[i][0] != sign * step:
                    continue
                for h in range(2):
                    field.shifted[Z_DIRS.index(i), plane, pl.ds(BASE + 8 * h, 8), :] = lane_shift(
                        field.raw[SLOT[i], plane, pl.ds(BASE + 8 * h, 8), :], sign * VELOCITY[i][2], lane
                    )

    def finish():
        for n, step in enumerate((1, -1)):
            pl.when(inside[step])(functools.partial(take, y_recv.at[:, n], send_sems.at[n]))
        take(post_raw.at[pl.ds(0, 10), pl.ds(0, 4), pl.ds(BASE, NY), :], send_sems.at[2])

    def shift_own(field):
        @pl.loop(0, NX // 4)
        def _(block):
            values = []
            for i in Z_DIRS:
                for q in range(4):
                    for h in range(2):
                        at = (4 * block + q + 1, pl.ds(BASE + 8 * h, 8))
                        value = field.raw[SLOT[i], at[0], at[1], :]
                        values.append((i, at, lane_shift(value, field.sign * VELOCITY[i][2], lane)))
            for i, at, value in values:
                field.shifted[Z_DIRS.index(i), at[0], at[1], :] = value

    def moved(field, tile, which=range(19)):
        kind, at, h = tile
        values = []
        for i in which:
            step_x, step_y = field.sign * VELOCITY[i][0], field.sign * VELOCITY[i][1]
            ref, flat, slot = field.pick(i)
            if kind == "x":
                values.append(ref[slot, at + 1 - step_x, pl.ds(BASE + 8 * h - step_y, 8), :])
            else:
                start = (8 * h + 1 - step_x) * PITCH + BASE - step_y + at
                values.append(flat[slot, pl.ds(start, 8, stride=PITCH), :])
        return values

    def flat_of(ref):
        shape = ref.shape
        return ref.reshape(*shape[:-3], NX * NY, NZ)

    def own(ref, tile, *lead):
        kind, at, h = tile
        if kind == "x":
            return ref[(*lead, at, pl.ds(8 * h, 8), slice(None))]
        return flat_of(ref)[(*lead, pl.ds(8 * NY * h + at, 8, stride=NY), slice(None))]

    def share_of(tile):
        open_voxel = own(mask, tile) == 1
        return jnp.where(open_voxel, own(gray, tile), 1.0), open_voxel

    def products(parts, values, tile, which):
        for i, value in zip(which, moved(drop, tile, which)):
            index = (0, 1, 2)[VELOCITY[i][0]]
            term = values[i] * value
            parts[index] = term if parts[index] is None else parts[index] + term

    def late(tile):
        kind, at, h = tile
        at_end, at_half = (1 if at == 0 else -1), (1 if h == 0 else -1)
        steps = (at_end, at_half) if kind == "x" else (at_half, at_end)
        return [i for i in range(19) if VELOCITY[i][0] == steps[0] or VELOCITY[i][1] == steps[1]]

    def first_half(tile, left=()):
        kind, at, h = tile
        f = moved(post, tile)
        even, odd, cross, j, second, rho, u = state_of(f)
        share, open_voxel = share_of(tile)
        out, grade = pull_back(u, moved(cot, tile), share, (even, odd, cross, j, second, rho, f[0]))
        centre = jnp.where(open_voxel, grade, 0.0)
        parts = [centre, None, None]
        products(parts, out, tile, [i for i in range(19) if i not in left])
        for i in range(19):
            if kind == "x":
                pre_raw[SLOT[i], at + 1, pl.ds(BASE + 8 * h, 8), :] = out[i]
            else:
                start = (8 * h + 1) * PITCH + BASE + at
                pre.flat_raw[SLOT[i], pl.ds(start, 8, stride=PITCH), :] = out[i]
        return parts

    def rest_of(tile):
        kind, at, h = tile
        which = late(tile)
        values = {}
        for i in which:
            if kind == "x":
                values[i] = pre_raw[SLOT[i], at + 1, pl.ds(BASE + 8 * h, 8), :]
            else:
                start = (8 * h + 1) * PITCH + BASE + at
                values[i] = pre.flat_raw[SLOT[i], pl.ds(start, 8, stride=PITCH), :]
        parts = [None, None, None]
        products(parts, values, tile, which)
        return parts

    def second_half(tile):
        kind, at, h = tile
        share, _ = share_of(tile)
        out, _ = pull_back([own(speed, tile, a) for a in range(3)], moved(pre, tile), share)
        for i in range(19):
            if kind == "x":
                out_ref[i, at, pl.ds(8 * h, 8), :] = out[i]
            else:
                flat_of(out_ref)[i, pl.ds(8 * NY * h + at, 8, stride=NY), :] = out[i]

    def laid(tile, place):
        return jnp.where(lane == place, jnp.sum(tile, axis=1, keepdims=True), 0.0)

    def without_edge(h, value):
        return jnp.where(row_at == 7 * h, 0.0, value)

    for load in side_loads:
        load.wait()

    def first_collision(x):
        for h in range(2):
            tile = ("x", x, h)
            share, open_voxel = share_of(tile)
            made, lost, u = collide([own(pop, tile, i) for i in range(19)], share, open_voxel)
            for i in range(19):
                post_raw[SLOT[i], x + 1, pl.ds(BASE + 8 * h, 8), :] = made[i]
                drop_raw[SLOT[i], x + 1, pl.ds(BASE + 8 * h, 8), :] = lost[i]
            for a in range(3):
                speed[a, x, pl.ds(8 * h, 8), :] = u[a]

    for c in range(CHUNKS):
        pop_loads[c].wait()

        @pl.loop(chunk * c, chunk * (c + 1))
        def _(x):
            first_collision(x)

    pack(post)
    pl.semaphore_wait(barrier, 2 + 3 * count_at(1) + count_at(2))
    post_across, post_along = copies(post)
    send(*post_across)
    take(cot_raw.at[:, pl.ds(1, NX), pl.ds(BASE, NY), :], in_sems.at[CHUNKS + 2])
    pack(cot)
    cot_across, cot_along = copies(cot)
    send(*cot_across, *post_along, *cot_along)
    tell(0)
    pack(drop)
    drop_across, drop_along = copies(drop)
    send(*drop_across, *drop_along)
    shift_own(post)
    shift_own(cot)
    hear(0)
    tell(1)
    shift_own(drop)

    @pl.loop(1, NX - 1)
    def _(x):
        halves = [[without_edge(h, part) for part in first_half(("x", x, h))] for h in range(2)]
        for q in range(3):
            grades[q, x] = halves[0][q] + halves[1][q]

    line = jnp.zeros((8, NZ), jnp.float32)
    for plane in range(NX):
        terms = [grades[q, x] for q, x in enumerate((plane, plane + 1, plane - 1)) if 0 < x < NX - 1]
        line = line + laid(functools.reduce(jnp.add, terms), plane + 1)
    line_ref[...] = line
    hear(1)
    tell(2)
    arrive(post, cot)
    receive(cot)
    receive(post)

    for end in (0, 1):
        at = (NX - 1) * end
        halves = [first_half(("x", at, h), late(("x", at, h))) for h in range(2)]
        for q in range(3):
            both = [part[q] for part in halves if part[q] is not None]
            grades[q, at] = functools.reduce(jnp.add, both) if both else jnp.zeros((8, NZ), jnp.float32)
        for h in range(2):
            for q, part in enumerate(first_half(("y", at, h), late(("y", at, h)))):
                kept = jnp.zeros((8, NZ), jnp.float32) if part is None else without_edge(h, part)
                y_grades[end, q, pl.ds(8 * h, 8), :] = kept

    pack(pre)
    pre_across, pre_along = copies(pre)
    send(*pre_across, *pre_along)
    arrive(drop)
    receive(drop)
    for end in (0, 1):
        at = (NX - 1) * end
        shares = [rest_of(("x", at, h)) for h in range(2)]
        for q in range(3):
            both = [part[q] for part in shares if part[q] is not None]
            if both:
                grades[q, at] += functools.reduce(jnp.add, both)
        for h in range(2):
            for q, part in enumerate(rest_of(("y", at, h))):
                if part is not None:
                    y_grades[end, q, pl.ds(8 * h, 8), :] += without_edge(h, part)

    line = line_ref[...]
    for q, lead in enumerate((1, 0, 2)):
        for at in (0, NX - 1):
            line = line + laid(grades[q, at], at + lead)
        for h in range(2):
            part = y_grades[0, q, pl.ds(8 * h, 8), :] + y_grades[1, q, pl.ds(8 * h, 8), :]
            line = line + laid(part, row_at + (8 * h + lead))
    rows[0, sp] = jnp.sum(line, axis=0, keepdims=True)
    hear(2)
    for side, step in peers:
        pltpu.make_async_remote_copy(
            src_ref=rows.at[0, sp],
            dst_ref=rows.at[side, sp],
            send_sem=row_sems.at[0],
            recv_sem=row_sems.at[1],
            device_id=peer(side, step),
        ).start()

    shift_own(pre)

    @pl.loop(1, NX - 1)
    def _(x):
        for h in range(2):
            second_half(("x", x, h))

    arrive(pre)
    receive(pre)

    @pl.loop(0, 2)
    def _(end):
        at = (NX - 1) * end
        for h in range(2):
            second_half(("x", at, h))
        for h in range(2):
            second_half(("y", at, h))

    finish()
    all_rows = rows.reshape(3 * spans, 1, NZ).at[pl.ds(0, len(peers))]
    take(all_rows, row_sems.at[1])
    one_lane = lax.broadcasted_iota(jnp.int32, (1, NZ), 1)
    total = jnp.sum(rows[0], axis=0)
    from_down = jnp.sum(rows[1], axis=0)
    from_up = jnp.sum(rows[2], axis=0)
    total = total + jnp.where(one_lane == 1, pltpu.roll(from_down, NZ - NX, 1), 0.0)
    total = total + jnp.where(one_lane == NX, pltpu.roll(from_up, NX, 1), 0.0)
    total = pltpu.roll(total, NZ - 1, 1) * (1.0 / math.sqrt(spans * NY * NZ))
    profile_ref[...] = total[:, :NX]
    take(all_rows, row_sems.at[0])


def local(flows, spans, populations, gray, fluid_mask, cotangent):
    def vmem(*shape):
        return pltpu.VMEM(shape, jnp.float32)

    zs = len(Z_DIRS)
    adjoint, profile = pl.pallas_call(
        functools.partial(kernel, flows, spans),
        out_shape=(
            jax.ShapeDtypeStruct((19, NX, NY, NZ), jnp.float32),
            jax.ShapeDtypeStruct((1, NX), jnp.float32),
        ),
        in_specs=[pl.BlockSpec(memory_space=pl.ANY)] * 4,
        out_specs=(pl.BlockSpec(memory_space=pltpu.VMEM), pl.BlockSpec(memory_space=pltpu.VMEM)),
        scratch_shapes=[
            vmem(19, NX, NY, NZ),
            vmem(NX, NY, NZ),
            pltpu.VMEM((NX, NY, NZ), jnp.int32),
            vmem(3, NX, NY, NZ),
            *[vmem(19, NX + 2, PITCH, NZ), vmem(zs, NX + 2, PITCH, NZ)] * 4,
            vmem(4, 2, 5, NX, NZ),
            vmem(4, 2, 6, NX, NZ),
            vmem(3, NX, 8, NZ),
            vmem(2, 3, NX, NZ),
            vmem(8, NZ),
            vmem(3, spans, 1, NZ),
            pltpu.SemaphoreType.DMA((CHUNKS + 3,)),
            pltpu.SemaphoreType.REGULAR((3,)),
            pltpu.SemaphoreType.DMA((3,)),
            pltpu.SemaphoreType.DMA((3, 3)),
            pltpu.SemaphoreType.DMA((2,)),
        ],
        compiler_params=pltpu.CompilerParams(
            collective_id=0, has_side_effects=True, vmem_limit_bytes=44 * 1024 * 1024
        ),
    )(*[pltpu.with_memory_space_constraint(x, pltpu.HBM) for x in (populations, gray, fluid_mask, cotangent)])
    return adjoint, profile.reshape(NX)


def solution(mesh):
    placed = (
        P(None, "flow", "span", None),
        P("flow", "span", None),
        P("flow", "span", None),
        P(None, "flow", "span", None),
    )
    return jax.shard_map(
        functools.partial(local, mesh.shape["flow"], mesh.shape["span"]),
        mesh=mesh,
        in_specs=placed,
        out_specs=(P(None, "flow", "span", None), P("flow")),
        check_vma=False,
    )
```

```python
import functools
import math

import jax
import jax.numpy as jnp
from jax import lax
from jax.experimental import pallas as pl
from jax.experimental.pallas import tpu as pltpu
from jax.sharding import PartitionSpec as P

VELOCITY = (
    (0, 0, 0),
    (1, 0, 0), (-1, 0, 0), (0, 1, 0), (0, -1, 0), (0, 0, 1), (0, 0, -1),
    (1, 1, 0), (-1, -1, 0), (1, -1, 0), (-1, 1, 0),
    (1, 0, 1), (-1, 0, -1), (1, 0, -1), (-1, 0, 1),
    (0, 1, 1), (0, -1, -1), (0, 1, -1), (0, -1, 1),
)
ORDER = (1, 7, 9, 11, 13, 2, 8, 10, 12, 14, 0, 3, 4, 5, 6, 15, 16, 17, 18)
SLOT = tuple(ORDER.index(i) for i in range(19))
X_GROUP = {1: 0, -1: 5}
Y_GROUP = {s: tuple(i for i in range(19) if VELOCITY[i][1] == s) for s in (1, -1)}
CORNER = {(1, 1): 7, (-1, -1): 8, (1, -1): 9, (-1, 1): 10}
PAIRS = ((1, 2), (3, 4), (5, 6), (7, 8), (9, 10), (11, 12), (13, 14), (15, 16), (17, 18))
RATE = 1.0 / 0.6 - 1.2
ENDS = ((0, 1), (0, 2), (1, 2))
Z_DIRS = tuple(i for i in range(19) if VELOCITY[i][2])
PITCH = 32
BASE = 8
NX = 16
NY = 16
NZ = 128
CHUNKS = 2


def split(f):
    even = [f[p] + f[m] for p, m in PAIRS]
    odd = [f[p] - f[m] for p, m in PAIRS]
    return even, odd


def sums(even, odd):
    plane = [even[3 + 2 * k] + even[4 + 2 * k] for k in range(3)]
    cross = [even[3 + 2 * k] - even[4 + 2 * k] for k in range(3)]
    plus = [odd[3 + 2 * k] + odd[4 + 2 * k] for k in range(3)]
    minus = [odd[3 + 2 * k] - odd[4 + 2 * k] for k in range(3)]
    first = [plus[0] + plus[1], minus[0] + plus[2], minus[1] + minus[2]]
    return plane, cross, first


def state_of(f):
    even, odd = split(f)
    plane, cross, first = sums(even, odd)
    j = [odd[a] + first[a] for a in range(3)]
    second = [even[0] + (plane[0] + plane[1]), even[1] + (plane[0] + plane[2]), even[2] + (plane[1] + plane[2])]
    rho = (f[0] + second[0]) + (even[1] + even[2]) + plane[2]
    inv = 1.0 / rho
    u = [entry * inv for entry in j]
    return even, odd, cross, j, second, rho, u


def join(even, odd):
    out = [None] * 19
    for k, (p, m) in enumerate(PAIRS):
        out[p] = even[k] + odd[k]
        out[m] = even[k] - odd[k]
    return out


def collide(f, share, open_voxel):
    even, odd, cross, j, second, rho, u = state_of(f)
    keep = 1.0 - share
    square = [j[a] * u[a] for a in range(3)]
    mixed = [j[0] * u[1], j[0] * u[2], j[1] * u[2]]
    base = rho - 1.5 * (square[0] + square[1] + square[2])
    third = rho * (1.0 / 3.0)
    lack = [second[a] - third - square[a] for a in range(3)]
    rest = 0.4 * base + RATE * (lack[0] + lack[1] + lack[2])
    base_axis = base * (1.0 / 15.0)
    base_edge = base * (1.0 / 30.0)
    grown = [0.15 * square[a] for a in range(3)]
    e_parts = [base_axis + 2.0 * grown[a] - (0.5 * RATE) * lack[a] for a in range(3)]
    o_parts = [0.2 * j[a] for a in range(3)]
    half = [0.1 * j[a] for a in range(3)]
    for k, (a, b) in enumerate(ENDS):
        common = base_edge + (grown[a] + grown[b])
        twist = (5.0 / 12.0) * mixed[k] - (0.25 * RATE) * cross[k]
        e_parts += [common + twist, common - twist]
        o_parts += [half[a] + half[b], half[a] - half[b]]
    drop = join(
        [jnp.where(open_voxel, 0.6 * even[k] - e_parts[k], 0.0) for k in range(9)],
        [jnp.where(open_voxel, -0.4 * odd[k] - o_parts[k], 0.0) for k in range(9)],
    )
    drop[0] = jnp.where(open_voxel, 1.2 * f[0] - rest, 0.0)
    post = [None] * 19
    post[0] = f[0] - keep * drop[0]
    for p, m in PAIRS:
        post[p] = f[m] - keep * drop[p]
        post[m] = f[p] - keep * drop[m]
    return post, drop, u


def pull_back(u, g, share, state=None):
    g_even, g_odd = split(g)
    g_plane, g_cross, g_first = sums(g_even, g_odd)
    keep = 1.0 - share
    k_even = 0.6 * share - 0.1
    k_odd = -0.4 * share - 0.1
    g_axes = g_even[0] + g_even[1] + g_even[2]
    g_edges = g_plane[0] + g_plane[1] + g_plane[2]
    weighted = g[0] * (1.0 / 3.0) + g_axes * (1.0 / 18.0) + g_edges * (1.0 / 36.0)
    both = [g_plane[0] + g_plane[1], g_plane[0] + g_plane[2], g_plane[1] + g_plane[2]]
    diag = [0.5 * g_even[a] - g[0] for a in range(3)]
    side = [0.25 * g_cross[k] for k in range(3)]
    flow = [0.2 * g_odd[a] + 0.1 * g_first[a] for a in range(3)]
    shared = 3.6 * weighted
    entry = [0.6 * g_even[a] + 0.3 * both[a] + (2.0 * RATE) * diag[a] - shared for a in range(3)]
    tilt = [(5.0 / 3.0) * side[k] for k in range(3)]
    turn = [
        u[0] * entry[0] + (tilt[0] * u[1] + tilt[1] * u[2]),
        u[1] * entry[1] + (tilt[0] * u[0] + tilt[2] * u[2]),
        u[2] * entry[2] + (tilt[1] * u[0] + tilt[2] * u[1]),
    ]
    scalar = 1.2 * weighted + (RATE / 3.0) * (diag[0] + diag[1] + diag[2])
    half_turn = [0.5 * turn[a] for a in range(3)]
    bar_rho = scalar - (u[0] * half_turn[0] + u[1] * half_turn[1] + u[2] * half_turn[2])
    grade = None
    if state is not None:
        even, odd, cross, j, second, rho, rest = state
        grade = 1.2 * (g[0] * rest) - rho * scalar
        for a in range(3):
            grade = grade - j[a] * (flow[a] + half_turn[a])
        bend = diag[0] * second[0] + diag[1] * second[1] + diag[2] * second[2]
        bend = bend + (side[0] * cross[0] + side[1] * cross[1] + side[2] * cross[2])
        dot_even = g_even[0] * even[0]
        dot_odd = g_odd[0] * odd[0]
        for k in range(1, 9):
            dot_even = dot_even + g_even[k] * even[k]
            dot_odd = dot_odd + g_odd[k] * odd[k]
        grade = grade + RATE * bend + (0.6 * dot_even - 0.4 * dot_odd)
    bar_rho = keep * bar_rho
    bar_j = [keep * (flow[a] + turn[a]) for a in range(3)]
    scale = keep * RATE
    diag = [scale * entry_a for entry_a in diag]
    side = [scale * entry_k for entry_k in side]
    e_parts = [bar_rho - diag[a] for a in range(3)]
    o_parts = list(bar_j)
    for k, (a, b) in enumerate(ENDS):
        common = e_parts[a] - diag[b]
        e_parts += [common - side[k], common + side[k]]
        o_parts += [bar_j[a] + bar_j[b], bar_j[a] - bar_j[b]]
    out = join(
        [k_even * g_even[k] + e_parts[k] for k in range(9)],
        [k_odd * g_odd[k] + o_parts[k] for k in range(9)],
    )
    out[0] = 2.0 * (k_even * g[0]) + bar_rho
    return out, grade


def lane_shift(value, step, lane):
    if step == 0:
        return value
    if step > 0:
        return jnp.where(lane == 0, 0.0, pltpu.roll(value, 1, 1))
    return jnp.where(lane == NZ - 1, 0.0, pltpu.roll(value, NZ - 1, 1))


class Field:
    def __init__(self, index, raw, shifted, y_send, y_recv, sign, recvs):
        self.index, self.raw, self.shifted = index, raw, shifted
        self.flat_raw = raw.reshape(19, (NX + 2) * PITCH, NZ)
        self.flat_shifted = shifted.reshape(len(Z_DIRS), (NX + 2) * PITCH, NZ)
        self.y_send, self.y_recv = y_send, y_recv
        self.sign, self.recvs = sign, recvs

    def pick(self, i):
        if VELOCITY[i][2]:
            return self.shifted, self.flat_shifted, Z_DIRS.index(i)
        return self.raw, self.flat_raw, SLOT[i]


def kernel(
    flows, spans,
    pop_hbm, gray_hbm, mask_hbm, cot_hbm,
    out_ref, profile_ref,
    pop, gray, mask, speed,
    post_raw, post_z, drop_raw, drop_z, cot_raw, cot_z, pre_raw, pre_z,
    y_send, y_recv, grades, y_grades, line_ref, rows,
    in_sems, far_sem, send_sems, recv_sems, row_sems,
):
    fl = lax.axis_index("flow")
    sp = lax.axis_index("span")
    up = lax.rem(fl + 1, flows)
    down = lax.rem(fl + flows - 1, flows)
    flow_at = {1: up, -1: down}
    span_at = {1: sp + 1, -1: sp - 1}
    inside = {1: sp < spans - 1, -1: sp > 0}
    post = Field(0, post_raw, post_z, y_send.at[0], y_recv.at[0], 1, recv_sems.at[0])
    cot = Field(1, cot_raw, cot_z, y_send.at[1], y_recv.at[1], -1, recv_sems.at[0])
    drop = Field(2, drop_raw, drop_z, y_send.at[2], y_recv.at[2], 1, recv_sems.at[1])
    pre = Field(3, pre_raw, pre_z, y_send.at[3], y_recv.at[3], -1, recv_sems.at[2])

    def target(step_x, step_y):
        return {
            "flow": flow_at[step_x] if step_x else fl,
            "span": span_at[step_y] if step_y else sp,
        }

    chunk = NX // CHUNKS
    pop_loads = [
        pltpu.make_async_copy(
            pop_hbm.at[:, pl.ds(chunk * c, chunk)], pop.at[:, pl.ds(chunk * c, chunk)], in_sems.at[c]
        )
        for c in range(CHUNKS)
    ]
    side_loads = [
        pltpu.make_async_copy(gray_hbm, gray, in_sems.at[CHUNKS]),
        pltpu.make_async_copy(mask_hbm, mask, in_sems.at[CHUNKS + 1]),
    ]
    cot_loads = [
        pltpu.make_async_copy(
            cot_hbm.at[ORDER[k]], cot_raw.at[k, pl.ds(1, NX), pl.ds(BASE, NY), :], in_sems.at[CHUNKS + 2]
        )
        for k in range(19)
    ]
    pop_loads[0].start()
    for load in side_loads + pop_loads[1:] + cot_loads:
        load.start()

    def take(ref, semaphore):
        pltpu.make_async_copy(ref, ref, semaphore).wait()

    steps = sorted(range(spans), key=lambda d: -min(d, spans - d))
    peers = [(side, step) for step in steps for side in (0, 1, 2) if side or step]

    def peer(side, step):
        return {"flow": (fl, up, down)[side], "span": lax.rem(sp + step, spans) if step else sp}

    order = sorted(range(spans), key=lambda s: (min(s % 8, 4), s))
    place_of = [order.index(s) for s in range(spans)]
    my_place = functools.reduce(jnp.add, [place_of[s] * (sp == s).astype(jnp.int32) for s in range(spans)])

    def far(s):
        return ((s - sp) * (s - sp) > 1).astype(jnp.int32)

    def before(s):
        return (my_place > place_of[s]).astype(jnp.int32) * far(s)

    def after(s):
        return (my_place < place_of[s]).astype(jnp.int32) * far(s)

    barrier = pltpu.get_barrier_semaphore()
    for step_x in (1, -1):
        pl.semaphore_signal(barrier, inc=1, device_id=target(step_x, 0))
    for step_y in (1, -1):

        @pl.when(inside[step_y])
        def _():
            for step_x in (1, -1, 0):
                pl.semaphore_signal(barrier, inc=1, device_id=target(step_x, step_y))

    for s in order[::-1]:

        @pl.when(after(s) == 1)
        def _():
            for side in (fl, up, down):
                pl.semaphore_signal(barrier, inc=1, device_id={"flow": side, "span": s})

    def count_at(distance):
        return (sp >= distance).astype(jnp.int32) + (sp + distance < spans).astype(jnp.int32)

    def tell():
        for s in order:

            @pl.when(before(s) == 1)
            def _():
                pl.semaphore_signal(far_sem, inc=1, device_id={"flow": fl, "span": s})

    def hear():
        later = functools.reduce(jnp.add, [after(s) for s in range(spans)])

        @pl.when(later > 0)
        def _():
            pl.semaphore_wait(far_sem, later)

    def copies(field):
        buf, sign = field.raw, field.sign
        across, along = [], []

        def remote(src, dst, index, where):
            return pltpu.make_async_remote_copy(
                src_ref=src,
                dst_ref=dst,
                send_sem=send_sems.at[index],
                recv_sem=field.recvs.at[index],
                device_id=where,
            )

        for n, step in enumerate((1, -1)):
            for m, step_x in enumerate((1, -1)):
                slot = SLOT[CORNER[(sign * step_x, sign * step)]]
                plane = NX if step_x > 0 else 1
                src = buf.at[slot, plane, pl.ds(BASE + (NY - 8 if step > 0 else 0), 8), :]
                dst = field.y_recv.at[n, 5, pl.ds(8 * m, 8), :]
                across.append((remote(src, dst, n, target(step_x, step)), inside[step]))
        for n, step in enumerate((1, -1)):
            src, dst = field.y_send.at[n], field.y_recv.at[n, pl.ds(0, 5)]
            across.append((remote(src, dst, n, target(0, step)), inside[step]))
        for n, step in enumerate((1, -1)):
            group = pl.ds(X_GROUP[sign * step], 5)
            src = buf.at[group, NX if step > 0 else 1, pl.ds(BASE, NY), :]
            dst = buf.at[group, 0 if step > 0 else NX + 1, pl.ds(BASE, NY), :]
            along.append((remote(src, dst, 2, target(step, 0)), None))
        return across, along

    def pack(field):
        for n, step in enumerate((1, -1)):
            row = PITCH + BASE + (NY - 1 if step > 0 else 0)
            for k, i in enumerate(Y_GROUP[field.sign * step]):
                field.y_send[n, k] = field.flat_raw[SLOT[i], pl.ds(row, NX, stride=PITCH), :]

    def send(*made):
        for copy, sent in made:
            if sent is None:
                copy.start()
            else:
                pl.when(sent)(copy.start)

    lane = lax.broadcasted_iota(jnp.int32, (8, NZ), 1)
    wide_lane = lax.broadcasted_iota(jnp.int32, (NX, NZ), 1)
    row_at = lax.broadcasted_iota(jnp.int32, (8, NZ), 0)

    def arrive(*fields):
        first, recvs = fields[0], fields[0].recvs
        for n, step in enumerate((1, -1)):
            came = y_recv.at[pl.ds(first.index, len(fields)), n]
            pl.when(inside[-step])(functools.partial(take, came, recvs.at[n]))
        take(first.raw.at[pl.ds(0, 10), pl.ds(0, len(fields)), pl.ds(BASE, NY), :], recvs.at[2])

    def receive(field):
        sign = field.sign
        for n, step in enumerate((1, -1)):
            row = PITCH + BASE + (-1 if step > 0 else NY)

            def place(step=step, n=n, row=row, empty=False):
                for k, i in enumerate(Y_GROUP[sign * step]):
                    _, flat, slot = field.pick(i)
                    if empty:
                        value = jnp.zeros((NX, NZ), jnp.float32)
                    else:
                        value = lane_shift(field.y_recv[n, k], sign * VELOCITY[i][2], wide_lane)
                    flat[slot, pl.ds(row, NX, stride=PITCH), :] = value
                for m, step_x in enumerate((1, -1)):
                    i = CORNER[(sign * step_x, sign * step)]
                    at = 8 * m + (7 if step > 0 else 0)
                    plane = 0 if step_x > 0 else NX + 1
                    corner = jnp.zeros((1, NZ), jnp.float32) if empty else field.y_recv[n, 5, pl.ds(at, 1), :]
                    field.raw[SLOT[i], plane, pl.ds(BASE + (-1 if step > 0 else NY), 1), :] = corner

            pl.when(inside[-step])(place)
            pl.when(jnp.logical_not(inside[-step]))(functools.partial(place, empty=True))
        for plane, step in ((0, 1), (NX + 1, -1)):
            for i in Z_DIRS:
                if VELOCITY[i][0] != sign * step:
                    continue
                for h in range(2):
                    field.shifted[Z_DIRS.index(i), plane, pl.ds(BASE + 8 * h, 8), :] = lane_shift(
                        field.raw[SLOT[i], plane, pl.ds(BASE + 8 * h, 8), :], sign * VELOCITY[i][2], lane
                    )

    def finish():
        for n, step in enumerate((1, -1)):
            pl.when(inside[step])(functools.partial(take, y_recv.at[:, n], send_sems.at[n]))
        take(post_raw.at[pl.ds(0, 10), pl.ds(0, 4), pl.ds(BASE, NY), :], send_sems.at[2])

    def shift_own(field):
        @pl.loop(0, NX // 4)
        def _(block):
            values = []
            for i in Z_DIRS:
                for q in range(4):
                    for h in range(2):
                        at = (4 * block + q + 1, pl.ds(BASE + 8 * h, 8))
                        value = field.raw[SLOT[i], at[0], at[1], :]
                        values.append((i, at, lane_shift(value, field.sign * VELOCITY[i][2], lane)))
            for i, at, value in values:
                field.shifted[Z_DIRS.index(i), at[0], at[1], :] = value

    def moved(field, tile, which=range(19)):
        kind, at, h = tile
        values = []
        for i in which:
            step_x, step_y = field.sign * VELOCITY[i][0], field.sign * VELOCITY[i][1]
            ref, flat, slot = field.pick(i)
            if kind == "x":
                values.append(ref[slot, at + 1 - step_x, pl.ds(BASE + 8 * h - step_y, 8), :])
            else:
                start = (8 * h + 1 - step_x) * PITCH + BASE - step_y + at
                values.append(flat[slot, pl.ds(start, 8, stride=PITCH), :])
        return values

    def flat_of(ref):
        shape = ref.shape
        return ref.reshape(*shape[:-3], NX * NY, NZ)

    def own(ref, tile, *lead):
        kind, at, h = tile
        if kind == "x":
            return ref[(*lead, at, pl.ds(8 * h, 8), slice(None))]
        return flat_of(ref)[(*lead, pl.ds(8 * NY * h + at, 8, stride=NY), slice(None))]

    def share_of(tile):
        open_voxel = own(mask, tile) == 1
        return jnp.where(open_voxel, own(gray, tile), 1.0), open_voxel

    def products(parts, values, tile, which):
        for i, value in zip(which, moved(drop, tile, which)):
            index = (0, 1, 2)[VELOCITY[i][0]]
            term = values[i] * value
            parts[index] = term if parts[index] is None else parts[index] + term

    def late(tile):
        kind, at, h = tile
        at_end, at_half = (1 if at == 0 else -1), (1 if h == 0 else -1)
        steps = (at_end, at_half) if kind == "x" else (at_half, at_end)
        return [i for i in range(19) if VELOCITY[i][0] == steps[0] or VELOCITY[i][1] == steps[1]]

    def first_half(tile, left=()):
        kind, at, h = tile
        f = moved(post, tile)
        even, odd, cross, j, second, rho, u = state_of(f)
        share, open_voxel = share_of(tile)
        out, grade = pull_back(u, moved(cot, tile), share, (even, odd, cross, j, second, rho, f[0]))
        centre = jnp.where(open_voxel, grade, 0.0)
        parts = [centre, None, None]
        products(parts, out, tile, [i for i in range(19) if i not in left])
        for i in range(19):
            if kind == "x":
                pre_raw[SLOT[i], at + 1, pl.ds(BASE + 8 * h, 8), :] = out[i]
            else:
                start = (8 * h + 1) * PITCH + BASE + at
                pre.flat_raw[SLOT[i], pl.ds(start, 8, stride=PITCH), :] = out[i]
        return parts

    def rest_of(tile):
        kind, at, h = tile
        which = late(tile)
        values = {}
        for i in which:
            if kind == "x":
                values[i] = pre_raw[SLOT[i], at + 1, pl.ds(BASE + 8 * h, 8), :]
            else:
                start = (8 * h + 1) * PITCH + BASE + at
                values[i] = pre.flat_raw[SLOT[i], pl.ds(start, 8, stride=PITCH), :]
        parts = [None, None, None]
        products(parts, values, tile, which)
        return parts

    def second_half(tile):
        kind, at, h = tile
        share, _ = share_of(tile)
        out, _ = pull_back([own(speed, tile, a) for a in range(3)], moved(pre, tile), share)
        for i in range(19):
            if kind == "x":
                out_ref[i, at, pl.ds(8 * h, 8), :] = out[i]
            else:
                flat_of(out_ref)[i, pl.ds(8 * NY * h + at, 8, stride=NY), :] = out[i]

    def laid(tile, place):
        return jnp.where(lane == place, jnp.sum(tile, axis=1, keepdims=True), 0.0)

    def without_edge(h, value):
        return jnp.where(row_at == 7 * h, 0.0, value)

    for load in side_loads:
        load.wait()

    def first_collision(x):
        for h in range(2):
            tile = ("x", x, h)
            share, open_voxel = share_of(tile)
            made, lost, u = collide([own(pop, tile, i) for i in range(19)], share, open_voxel)
            for i in range(19):
                post_raw[SLOT[i], x + 1, pl.ds(BASE + 8 * h, 8), :] = made[i]
                drop_raw[SLOT[i], x + 1, pl.ds(BASE + 8 * h, 8), :] = lost[i]
            for a in range(3):
                speed[a, x, pl.ds(8 * h, 8), :] = u[a]

    for c in range(CHUNKS):
        pop_loads[c].wait()

        @pl.loop(chunk * c, chunk * (c + 1))
        def _(x):
            first_collision(x)

    pack(post)
    pl.semaphore_wait(barrier, 2 + 3 * (count_at(1) + functools.reduce(jnp.add, [before(s) for s in range(spans)])))
    post_across, post_along = copies(post)
    send(*post_across)
    take(cot_raw.at[:, pl.ds(1, NX), pl.ds(BASE, NY), :], in_sems.at[CHUNKS + 2])
    pack(cot)
    cot_across, cot_along = copies(cot)
    send(*cot_across, *post_along, *cot_along)
    tell()
    pack(drop)
    drop_across, drop_along = copies(drop)
    send(*drop_across, *drop_along)
    shift_own(post)
    shift_own(cot)
    shift_own(drop)

    @pl.loop(1, NX - 1)
    def _(x):
        halves = [[without_edge(h, part) for part in first_half(("x", x, h))] for h in range(2)]
        for q in range(3):
            grades[q, x] = halves[0][q] + halves[1][q]

    line = jnp.zeros((8, NZ), jnp.float32)
    for plane in range(NX):
        terms = [grades[q, x] for q, x in enumerate((plane, plane + 1, plane - 1)) if 0 < x < NX - 1]
        line = line + laid(functools.reduce(jnp.add, terms), plane + 1)
    line_ref[...] = line
    arrive(post, cot)
    receive(cot)
    receive(post)

    for end in (0, 1):
        at = (NX - 1) * end
        halves = [first_half(("x", at, h), late(("x", at, h))) for h in range(2)]
        for q in range(3):
            both = [part[q] for part in halves if part[q] is not None]
            grades[q, at] = functools.reduce(jnp.add, both) if both else jnp.zeros((8, NZ), jnp.float32)
        for h in range(2):
            for q, part in enumerate(first_half(("y", at, h), late(("y", at, h)))):
                kept = jnp.zeros((8, NZ), jnp.float32) if part is None else without_edge(h, part)
                y_grades[end, q, pl.ds(8 * h, 8), :] = kept

    pack(pre)
    pre_across, pre_along = copies(pre)
    send(*pre_across, *pre_along)
    arrive(drop)
    receive(drop)
    for end in (0, 1):
        at = (NX - 1) * end
        shares = [rest_of(("x", at, h)) for h in range(2)]
        for q in range(3):
            both = [part[q] for part in shares if part[q] is not None]
            if both:
                grades[q, at] += functools.reduce(jnp.add, both)
        for h in range(2):
            for q, part in enumerate(rest_of(("y", at, h))):
                if part is not None:
                    y_grades[end, q, pl.ds(8 * h, 8), :] += without_edge(h, part)

    line = line_ref[...]
    for q, lead in enumerate((1, 0, 2)):
        for at in (0, NX - 1):
            line = line + laid(grades[q, at], at + lead)
        for h in range(2):
            part = y_grades[0, q, pl.ds(8 * h, 8), :] + y_grades[1, q, pl.ds(8 * h, 8), :]
            line = line + laid(part, row_at + (8 * h + lead))
    rows[0, sp] = jnp.sum(line, axis=0, keepdims=True)
    hear()
    for side, step in peers:
        pltpu.make_async_remote_copy(
            src_ref=rows.at[0, sp],
            dst_ref=rows.at[side, sp],
            send_sem=row_sems.at[0],
            recv_sem=row_sems.at[1],
            device_id=peer(side, step),
        ).start()

    shift_own(pre)

    @pl.loop(1, NX - 1)
    def _(x):
        for h in range(2):
            second_half(("x", x, h))

    arrive(pre)
    receive(pre)

    @pl.loop(0, 2)
    def _(end):
        at = (NX - 1) * end
        for h in range(2):
            second_half(("x", at, h))
        for h in range(2):
            second_half(("y", at, h))

    finish()
    all_rows = rows.reshape(3 * spans, 1, NZ).at[pl.ds(0, len(peers))]
    take(all_rows, row_sems.at[1])
    one_lane = lax.broadcasted_iota(jnp.int32, (1, NZ), 1)
    total = jnp.sum(rows[0], axis=0)
    from_down = jnp.sum(rows[1], axis=0)
    from_up = jnp.sum(rows[2], axis=0)
    total = total + jnp.where(one_lane == 1, pltpu.roll(from_down, NZ - NX, 1), 0.0)
    total = total + jnp.where(one_lane == NX, pltpu.roll(from_up, NX, 1), 0.0)
    total = pltpu.roll(total, NZ - 1, 1) * (1.0 / math.sqrt(spans * NY * NZ))
    profile_ref[...] = total[:, :NX]
    take(all_rows, row_sems.at[0])


def local(flows, spans, populations, gray, fluid_mask, cotangent):
    def vmem(*shape):
        return pltpu.VMEM(shape, jnp.float32)

    zs = len(Z_DIRS)
    adjoint, profile = pl.pallas_call(
        functools.partial(kernel, flows, spans),
        out_shape=(
            jax.ShapeDtypeStruct((19, NX, NY, NZ), jnp.float32),
            jax.ShapeDtypeStruct((1, NX), jnp.float32),
        ),
        in_specs=[pl.BlockSpec(memory_space=pl.ANY)] * 4,
        out_specs=(pl.BlockSpec(memory_space=pltpu.VMEM), pl.BlockSpec(memory_space=pltpu.VMEM)),
        scratch_shapes=[
            vmem(19, NX, NY, NZ),
            vmem(NX, NY, NZ),
            pltpu.VMEM((NX, NY, NZ), jnp.int32),
            vmem(3, NX, NY, NZ),
            *[vmem(19, NX + 2, PITCH, NZ), vmem(zs, NX + 2, PITCH, NZ)] * 4,
            vmem(4, 2, 5, NX, NZ),
            vmem(4, 2, 6, NX, NZ),
            vmem(3, NX, 8, NZ),
            vmem(2, 3, NX, NZ),
            vmem(8, NZ),
            vmem(3, spans, 1, NZ),
            pltpu.SemaphoreType.DMA((CHUNKS + 3,)),
            pltpu.SemaphoreType.REGULAR,
            pltpu.SemaphoreType.DMA((3,)),
            pltpu.SemaphoreType.DMA((3, 3)),
            pltpu.SemaphoreType.DMA((2,)),
        ],
        compiler_params=pltpu.CompilerParams(
            collective_id=0, has_side_effects=True, vmem_limit_bytes=44 * 1024 * 1024
        ),
    )(*[pltpu.with_memory_space_constraint(x, pltpu.HBM) for x in (populations, gray, fluid_mask, cotangent)])
    return adjoint, profile.reshape(NX)


def solution(mesh):
    placed = (
        P(None, "flow", "span", None),
        P("flow", "span", None),
        P("flow", "span", None),
        P(None, "flow", "span", None),
    )
    return jax.shard_map(
        functools.partial(local, mesh.shape["flow"], mesh.shape["span"]),
        mesh=mesh,
        in_specs=placed,
        out_specs=(P(None, "flow", "span", None), P("flow")),
        check_vma=False,
    )
```

```python
import functools
import math

import jax
import jax.numpy as jnp
from jax import lax
from jax.experimental import pallas as pl
from jax.experimental.pallas import tpu as pltpu
from jax.sharding import PartitionSpec as P

VELOCITY = (
    (0, 0, 0),
    (1, 0, 0), (-1, 0, 0), (0, 1, 0), (0, -1, 0), (0, 0, 1), (0, 0, -1),
    (1, 1, 0), (-1, -1, 0), (1, -1, 0), (-1, 1, 0),
    (1, 0, 1), (-1, 0, -1), (1, 0, -1), (-1, 0, 1),
    (0, 1, 1), (0, -1, -1), (0, 1, -1), (0, -1, 1),
)
ORDER = (1, 7, 9, 11, 13, 2, 8, 10, 12, 14, 0, 3, 4, 5, 6, 15, 16, 17, 18)
SLOT = tuple(ORDER.index(i) for i in range(19))
X_GROUP = {1: 0, -1: 5}
Y_GROUP = {s: tuple(i for i in range(19) if VELOCITY[i][1] == s) for s in (1, -1)}
CORNER = {(1, 1): 7, (-1, -1): 8, (1, -1): 9, (-1, 1): 10}
PAIRS = ((1, 2), (3, 4), (5, 6), (7, 8), (9, 10), (11, 12), (13, 14), (15, 16), (17, 18))
RATE = 1.0 / 0.6 - 1.2
ENDS = ((0, 1), (0, 2), (1, 2))
Z_DIRS = tuple(i for i in range(19) if VELOCITY[i][2])
PITCH = 32
BASE = 8
NX = 16
NY = 16
NZ = 128
CHUNKS = 2


def split(f):
    even = [f[p] + f[m] for p, m in PAIRS]
    odd = [f[p] - f[m] for p, m in PAIRS]
    return even, odd


def sums(even, odd):
    plane = [even[3 + 2 * k] + even[4 + 2 * k] for k in range(3)]
    cross = [even[3 + 2 * k] - even[4 + 2 * k] for k in range(3)]
    plus = [odd[3 + 2 * k] + odd[4 + 2 * k] for k in range(3)]
    minus = [odd[3 + 2 * k] - odd[4 + 2 * k] for k in range(3)]
    first = [plus[0] + plus[1], minus[0] + plus[2], minus[1] + minus[2]]
    return plane, cross, first


def state_of(f):
    even, odd = split(f)
    plane, cross, first = sums(even, odd)
    j = [odd[a] + first[a] for a in range(3)]
    second = [even[0] + (plane[0] + plane[1]), even[1] + (plane[0] + plane[2]), even[2] + (plane[1] + plane[2])]
    rho = (f[0] + second[0]) + (even[1] + even[2]) + plane[2]
    inv = 1.0 / rho
    u = [entry * inv for entry in j]
    return even, odd, cross, j, second, rho, u


def join(even, odd):
    out = [None] * 19
    for k, (p, m) in enumerate(PAIRS):
        out[p] = even[k] + odd[k]
        out[m] = even[k] - odd[k]
    return out


def collide(f, share, open_voxel):
    even, odd, cross, j, second, rho, u = state_of(f)
    keep = 1.0 - share
    square = [j[a] * u[a] for a in range(3)]
    mixed = [j[0] * u[1], j[0] * u[2], j[1] * u[2]]
    base = rho - 1.5 * (square[0] + square[1] + square[2])
    third = rho * (1.0 / 3.0)
    lack = [second[a] - third - square[a] for a in range(3)]
    rest = 0.4 * base + RATE * (lack[0] + lack[1] + lack[2])
    base_axis = base * (1.0 / 15.0)
    base_edge = base * (1.0 / 30.0)
    grown = [0.15 * square[a] for a in range(3)]
    e_parts = [base_axis + 2.0 * grown[a] - (0.5 * RATE) * lack[a] for a in range(3)]
    o_parts = [0.2 * j[a] for a in range(3)]
    half = [0.1 * j[a] for a in range(3)]
    for k, (a, b) in enumerate(ENDS):
        common = base_edge + (grown[a] + grown[b])
        twist = (5.0 / 12.0) * mixed[k] - (0.25 * RATE) * cross[k]
        e_parts += [common + twist, common - twist]
        o_parts += [half[a] + half[b], half[a] - half[b]]
    drop = join(
        [jnp.where(open_voxel, 0.6 * even[k] - e_parts[k], 0.0) for k in range(9)],
        [jnp.where(open_voxel, -0.4 * odd[k] - o_parts[k], 0.0) for k in range(9)],
    )
    drop[0] = jnp.where(open_voxel, 1.2 * f[0] - rest, 0.0)
    post = [None] * 19
    post[0] = f[0] - keep * drop[0]
    for p, m in PAIRS:
        post[p] = f[m] - keep * drop[p]
        post[m] = f[p] - keep * drop[m]
    return post, drop, u


def pull_back(u, g, share, state=None):
    g_even, g_odd = split(g)
    g_plane, g_cross, g_first = sums(g_even, g_odd)
    keep = 1.0 - share
    k_even = 0.6 * share - 0.1
    k_odd = -0.4 * share - 0.1
    g_axes = g_even[0] + g_even[1] + g_even[2]
    g_edges = g_plane[0] + g_plane[1] + g_plane[2]
    weighted = g[0] * (1.0 / 3.0) + g_axes * (1.0 / 18.0) + g_edges * (1.0 / 36.0)
    both = [g_plane[0] + g_plane[1], g_plane[0] + g_plane[2], g_plane[1] + g_plane[2]]
    diag = [0.5 * g_even[a] - g[0] for a in range(3)]
    side = [0.25 * g_cross[k] for k in range(3)]
    flow = [0.2 * g_odd[a] + 0.1 * g_first[a] for a in range(3)]
    shared = 3.6 * weighted
    entry = [0.6 * g_even[a] + 0.3 * both[a] + (2.0 * RATE) * diag[a] - shared for a in range(3)]
    tilt = [(5.0 / 3.0) * side[k] for k in range(3)]
    turn = [
        u[0] * entry[0] + (tilt[0] * u[1] + tilt[1] * u[2]),
        u[1] * entry[1] + (tilt[0] * u[0] + tilt[2] * u[2]),
        u[2] * entry[2] + (tilt[1] * u[0] + tilt[2] * u[1]),
    ]
    scalar = 1.2 * weighted + (RATE / 3.0) * (diag[0] + diag[1] + diag[2])
    half_turn = [0.5 * turn[a] for a in range(3)]
    bar_rho = scalar - (u[0] * half_turn[0] + u[1] * half_turn[1] + u[2] * half_turn[2])
    grade = None
    if state is not None:
        even, odd, cross, j, second, rho, rest = state
        grade = 1.2 * (g[0] * rest) - rho * scalar
        for a in range(3):
            grade = grade - j[a] * (flow[a] + half_turn[a])
        bend = diag[0] * second[0] + diag[1] * second[1] + diag[2] * second[2]
        bend = bend + (side[0] * cross[0] + side[1] * cross[1] + side[2] * cross[2])
        dot_even = g_even[0] * even[0]
        dot_odd = g_odd[0] * odd[0]
        for k in range(1, 9):
            dot_even = dot_even + g_even[k] * even[k]
            dot_odd = dot_odd + g_odd[k] * odd[k]
        grade = grade + RATE * bend + (0.6 * dot_even - 0.4 * dot_odd)
    bar_rho = keep * bar_rho
    bar_j = [keep * (flow[a] + turn[a]) for a in range(3)]
    scale = keep * RATE
    diag = [scale * entry_a for entry_a in diag]
    side = [scale * entry_k for entry_k in side]
    e_parts = [bar_rho - diag[a] for a in range(3)]
    o_parts = list(bar_j)
    for k, (a, b) in enumerate(ENDS):
        common = e_parts[a] - diag[b]
        e_parts += [common - side[k], common + side[k]]
        o_parts += [bar_j[a] + bar_j[b], bar_j[a] - bar_j[b]]
    out = join(
        [k_even * g_even[k] + e_parts[k] for k in range(9)],
        [k_odd * g_odd[k] + o_parts[k] for k in range(9)],
    )
    out[0] = 2.0 * (k_even * g[0]) + bar_rho
    return out, grade


def lane_shift(value, step, lane):
    if step == 0:
        return value
    if step > 0:
        return jnp.where(lane == 0, 0.0, pltpu.roll(value, 1, 1))
    return jnp.where(lane == NZ - 1, 0.0, pltpu.roll(value, NZ - 1, 1))


class Field:
    def __init__(self, index, raw, shifted, y_send, y_recv, sign, recvs):
        self.index, self.raw, self.shifted = index, raw, shifted
        self.flat_raw = raw.reshape(19, (NX + 2) * PITCH, NZ)
        self.flat_shifted = shifted.reshape(len(Z_DIRS), (NX + 2) * PITCH, NZ)
        self.y_send, self.y_recv = y_send, y_recv
        self.sign, self.recvs = sign, recvs

    def pick(self, i):
        if VELOCITY[i][2]:
            return self.shifted, self.flat_shifted, Z_DIRS.index(i)
        return self.raw, self.flat_raw, SLOT[i]


def kernel(
    flows, spans,
    pop_hbm, gray_hbm, mask_hbm, cot_hbm,
    out_ref, profile_ref,
    pop, gray, mask, speed,
    post_raw, post_z, drop_raw, drop_z, cot_raw, cot_z, pre_raw, pre_z,
    y_send, y_recv, dense, grades, y_grades, line_ref, rows,
    in_sems, far_sem, send_sems, recv_sems, row_sems,
):
    fl = lax.axis_index("flow")
    sp = lax.axis_index("span")
    up = lax.rem(fl + 1, flows)
    down = lax.rem(fl + flows - 1, flows)
    flow_at = {1: up, -1: down}
    span_at = {1: sp + 1, -1: sp - 1}
    inside = {1: sp < spans - 1, -1: sp > 0}
    post = Field(0, post_raw, post_z, y_send.at[0], y_recv.at[0], 1, recv_sems.at[0])
    cot = Field(1, cot_raw, cot_z, y_send.at[1], y_recv.at[1], -1, recv_sems.at[0])
    drop = Field(2, drop_raw, drop_z, y_send.at[2], y_recv.at[2], 1, recv_sems.at[1])
    pre = Field(3, pre_raw, pre_z, y_send.at[3], y_recv.at[3], -1, recv_sems.at[2])

    def target(step_x, step_y):
        return {
            "flow": flow_at[step_x] if step_x else fl,
            "span": span_at[step_y] if step_y else sp,
        }

    chunk = NX // CHUNKS
    pop_loads = [
        pltpu.make_async_copy(
            pop_hbm.at[:, pl.ds(chunk * c, chunk)], pop.at[:, pl.ds(chunk * c, chunk)], in_sems.at[c]
        )
        for c in range(CHUNKS)
    ]
    side_loads = [
        pltpu.make_async_copy(gray_hbm, gray, in_sems.at[CHUNKS]),
        pltpu.make_async_copy(mask_hbm, mask, in_sems.at[CHUNKS + 1]),
    ]
    cot_loads = [
        pltpu.make_async_copy(
            cot_hbm.at[ORDER[k]], cot_raw.at[k, pl.ds(1, NX), pl.ds(BASE, NY), :], in_sems.at[CHUNKS + 2]
        )
        for k in range(19)
    ]
    pop_loads[0].start()
    for load in side_loads + pop_loads[1:] + cot_loads:
        load.start()

    def take(ref, semaphore):
        pltpu.make_async_copy(ref, ref, semaphore).wait()

    steps = sorted(range(spans), key=lambda d: -min(d, spans - d))
    peers = [(side, step) for step in steps for side in (0, 1, 2) if side or step]

    def peer(side, step):
        return {"flow": (fl, up, down)[side], "span": lax.rem(sp + step, spans) if step else sp}

    order = sorted(range(spans), key=lambda s: (min(s % 8, 4), s))
    place_of = [order.index(s) for s in range(spans)]
    my_place = functools.reduce(jnp.add, [place_of[s] * (sp == s).astype(jnp.int32) for s in range(spans)])

    def far(s):
        return ((s - sp) * (s - sp) > 1).astype(jnp.int32)

    def before(s):
        return (my_place > place_of[s]).astype(jnp.int32) * far(s)

    def after(s):
        return (my_place < place_of[s]).astype(jnp.int32) * far(s)

    barrier = pltpu.get_barrier_semaphore()
    for step_x in (1, -1):
        pl.semaphore_signal(barrier, inc=1, device_id=target(step_x, 0))
    for step_y in (1, -1):

        @pl.when(inside[step_y])
        def _():
            for step_x in (1, -1, 0):
                pl.semaphore_signal(barrier, inc=1, device_id=target(step_x, step_y))

    for s in order[::-1]:

        @pl.when(after(s) == 1)
        def _():
            for side in (fl, up, down):
                pl.semaphore_signal(barrier, inc=1, device_id={"flow": side, "span": s})

    def count_at(distance):
        return (sp >= distance).astype(jnp.int32) + (sp + distance < spans).astype(jnp.int32)

    def tell():
        for s in order:

            @pl.when(before(s) == 1)
            def _():
                pl.semaphore_signal(far_sem, inc=1, device_id={"flow": fl, "span": s})

    def hear():
        later = functools.reduce(jnp.add, [after(s) for s in range(spans)])

        @pl.when(later > 0)
        def _():
            pl.semaphore_wait(far_sem, later)

    def copies(field):
        buf, sign = field.raw, field.sign
        across, along = [], []

        def remote(src, dst, index, where):
            return pltpu.make_async_remote_copy(
                src_ref=src,
                dst_ref=dst,
                send_sem=send_sems.at[index],
                recv_sem=field.recvs.at[index],
                device_id=where,
            )

        for n, step in enumerate((1, -1)):
            for m, step_x in enumerate((1, -1)):
                slot = SLOT[CORNER[(sign * step_x, sign * step)]]
                plane = NX if step_x > 0 else 1
                src = buf.at[slot, plane, pl.ds(BASE + (NY - 8 if step > 0 else 0), 8), :]
                dst = field.y_recv.at[n, 5, pl.ds(8 * m, 8), :]
                across.append((remote(src, dst, n, target(step_x, step)), inside[step]))
        for n, step in enumerate((1, -1)):
            src, dst = field.y_send.at[n], field.y_recv.at[n, pl.ds(0, 5)]
            across.append((remote(src, dst, n, target(0, step)), inside[step]))
        for n, step in enumerate((1, -1)):
            group = pl.ds(X_GROUP[sign * step], 5)
            src = buf.at[group, NX if step > 0 else 1, pl.ds(BASE, NY), :]
            dst = buf.at[group, 0 if step > 0 else NX + 1, pl.ds(BASE, NY), :]
            along.append((remote(src, dst, 2, target(step, 0)), None))
        return across, along

    def pack(field):
        for n, step in enumerate((1, -1)):
            row = PITCH + BASE + (NY - 1 if step > 0 else 0)
            for k, i in enumerate(Y_GROUP[field.sign * step]):
                field.y_send[n, k] = field.flat_raw[SLOT[i], pl.ds(row, NX, stride=PITCH), :]

    def send(*made):
        for copy, sent in made:
            if sent is None:
                copy.start()
            else:
                pl.when(sent)(copy.start)

    lane = lax.broadcasted_iota(jnp.int32, (8, NZ), 1)
    wide_lane = lax.broadcasted_iota(jnp.int32, (NX, NZ), 1)
    row_at = lax.broadcasted_iota(jnp.int32, (8, NZ), 0)

    def arrive(*fields):
        first, recvs = fields[0], fields[0].recvs
        for n, step in enumerate((1, -1)):
            came = y_recv.at[pl.ds(first.index, len(fields)), n]
            pl.when(inside[-step])(functools.partial(take, came, recvs.at[n]))
        take(first.raw.at[pl.ds(0, 10), pl.ds(0, len(fields)), pl.ds(BASE, NY), :], recvs.at[2])

    def receive(field):
        sign = field.sign
        for n, step in enumerate((1, -1)):
            row = PITCH + BASE + (-1 if step > 0 else NY)

            def place(step=step, n=n, row=row, empty=False):
                for k, i in enumerate(Y_GROUP[sign * step]):
                    _, flat, slot = field.pick(i)
                    if empty:
                        value = jnp.zeros((NX, NZ), jnp.float32)
                    else:
                        value = lane_shift(field.y_recv[n, k], sign * VELOCITY[i][2], wide_lane)
                    flat[slot, pl.ds(row, NX, stride=PITCH), :] = value
                    if field.index < 2:
                        dense[field.index, n, i, pl.ds(BASE, NX), :] = value
                for m, step_x in enumerate((1, -1)):
                    i = CORNER[(sign * step_x, sign * step)]
                    at = 8 * m + (7 if step > 0 else 0)
                    plane = 0 if step_x > 0 else NX + 1
                    corner = jnp.zeros((1, NZ), jnp.float32) if empty else field.y_recv[n, 5, pl.ds(at, 1), :]
                    field.raw[SLOT[i], plane, pl.ds(BASE + (-1 if step > 0 else NY), 1), :] = corner

            pl.when(inside[-step])(place)
            pl.when(jnp.logical_not(inside[-step]))(functools.partial(place, empty=True))
        for plane, step in ((0, 1), (NX + 1, -1)):
            for i in Z_DIRS:
                if VELOCITY[i][0] != sign * step:
                    continue
                for h in range(2):
                    field.shifted[Z_DIRS.index(i), plane, pl.ds(BASE + 8 * h, 8), :] = lane_shift(
                        field.raw[SLOT[i], plane, pl.ds(BASE + 8 * h, 8), :], sign * VELOCITY[i][2], lane
                    )

    def finish():
        for n, step in enumerate((1, -1)):
            pl.when(inside[step])(functools.partial(take, y_recv.at[:, n], send_sems.at[n]))
        take(post_raw.at[pl.ds(0, 10), pl.ds(0, 4), pl.ds(BASE, NY), :], send_sems.at[2])

    def shift_own(field):
        @pl.loop(0, NX // 4)
        def _(block):
            values = []
            for i in Z_DIRS:
                for q in range(4):
                    for h in range(2):
                        at = (4 * block + q + 1, pl.ds(BASE + 8 * h, 8))
                        value = field.raw[SLOT[i], at[0], at[1], :]
                        values.append((i, at, lane_shift(value, field.sign * VELOCITY[i][2], lane)))
            for i, at, value in values:
                field.shifted[Z_DIRS.index(i), at[0], at[1], :] = value

    def gather(field):
        for end in (0, 1):
            for i in range(19):
                step_y = field.sign * VELOCITY[i][1]
                if step_y == 1 - 2 * end:
                    continue
                _, flat, slot = field.pick(i)
                row = PITCH + BASE + (NY - 1) * end - step_y
                dense[field.index, end, i, pl.ds(BASE, NX), :] = flat[slot, pl.ds(row, NX, stride=PITCH), :]

    def moved(field, tile, which=range(19)):
        kind, at, h = tile
        values = []
        for i in which:
            step_x, step_y = field.sign * VELOCITY[i][0], field.sign * VELOCITY[i][1]
            ref, flat, slot = field.pick(i)
            if kind == "x":
                values.append(ref[slot, at + 1 - step_x, pl.ds(BASE + 8 * h - step_y, 8), :])
            elif field.index < 2:
                values.append(dense[field.index, int(at > 0), i, pl.ds(BASE + 8 * h - step_x, 8), :])
            else:
                start = (8 * h + 1 - step_x) * PITCH + BASE - step_y + at
                values.append(flat[slot, pl.ds(start, 8, stride=PITCH), :])
        return values

    def flat_of(ref):
        shape = ref.shape
        return ref.reshape(*shape[:-3], NX * NY, NZ)

    def own(ref, tile, *lead):
        kind, at, h = tile
        if kind == "x":
            return ref[(*lead, at, pl.ds(8 * h, 8), slice(None))]
        return flat_of(ref)[(*lead, pl.ds(8 * NY * h + at, 8, stride=NY), slice(None))]

    def share_of(tile):
        open_voxel = own(mask, tile) == 1
        return jnp.where(open_voxel, own(gray, tile), 1.0), open_voxel

    def products(parts, values, tile, which):
        for i, value in zip(which, moved(drop, tile, which)):
            index = (0, 1, 2)[VELOCITY[i][0]]
            term = values[i] * value
            parts[index] = term if parts[index] is None else parts[index] + term

    def late(tile):
        kind, at, h = tile
        at_end, at_half = (1 if at == 0 else -1), (1 if h == 0 else -1)
        steps = (at_end, at_half) if kind == "x" else (at_half, at_end)
        return [i for i in range(19) if VELOCITY[i][0] == steps[0] or VELOCITY[i][1] == steps[1]]

    def first_half(tile, left=()):
        kind, at, h = tile
        f = moved(post, tile)
        even, odd, cross, j, second, rho, u = state_of(f)
        share, open_voxel = share_of(tile)
        out, grade = pull_back(u, moved(cot, tile), share, (even, odd, cross, j, second, rho, f[0]))
        centre = jnp.where(open_voxel, grade, 0.0)
        parts = [centre, None, None]
        products(parts, out, tile, [i for i in range(19) if i not in left])
        for i in range(19):
            if kind == "x":
                pre_raw[SLOT[i], at + 1, pl.ds(BASE + 8 * h, 8), :] = out[i]
            else:
                start = (8 * h + 1) * PITCH + BASE + at
                pre.flat_raw[SLOT[i], pl.ds(start, 8, stride=PITCH), :] = out[i]
        return parts

    def rest_of(tile):
        kind, at, h = tile
        which = late(tile)
        values = {}
        for i in which:
            if kind == "x":
                values[i] = pre_raw[SLOT[i], at + 1, pl.ds(BASE + 8 * h, 8), :]
            else:
                start = (8 * h + 1) * PITCH + BASE + at
                values[i] = pre.flat_raw[SLOT[i], pl.ds(start, 8, stride=PITCH), :]
        parts = [None, None, None]
        products(parts, values, tile, which)
        return parts

    def second_half(tile):
        kind, at, h = tile
        share, _ = share_of(tile)
        out, _ = pull_back([own(speed, tile, a) for a in range(3)], moved(pre, tile), share)
        for i in range(19):
            if kind == "x":
                out_ref[i, at, pl.ds(8 * h, 8), :] = out[i]
            else:
                flat_of(out_ref)[i, pl.ds(8 * NY * h + at, 8, stride=NY), :] = out[i]

    def laid(tile, place):
        return jnp.where(lane == place, jnp.sum(tile, axis=1, keepdims=True), 0.0)

    def without_edge(h, value):
        return jnp.where(row_at == 7 * h, 0.0, value)

    for load in side_loads:
        load.wait()

    def first_collision(x):
        for h in range(2):
            tile = ("x", x, h)
            share, open_voxel = share_of(tile)
            made, lost, u = collide([own(pop, tile, i) for i in range(19)], share, open_voxel)
            for i in range(19):
                post_raw[SLOT[i], x + 1, pl.ds(BASE + 8 * h, 8), :] = made[i]
                drop_raw[SLOT[i], x + 1, pl.ds(BASE + 8 * h, 8), :] = lost[i]
            for a in range(3):
                speed[a, x, pl.ds(8 * h, 8), :] = u[a]

    for c in range(CHUNKS):
        pop_loads[c].wait()

        @pl.loop(chunk * c, chunk * (c + 1))
        def _(x):
            first_collision(x)

    pack(post)
    pl.semaphore_wait(barrier, 2 + 3 * (count_at(1) + functools.reduce(jnp.add, [before(s) for s in range(spans)])))
    post_across, post_along = copies(post)
    send(*post_across)
    take(cot_raw.at[:, pl.ds(1, NX), pl.ds(BASE, NY), :], in_sems.at[CHUNKS + 2])
    pack(cot)
    cot_across, cot_along = copies(cot)
    send(*cot_across, *post_along, *cot_along)
    tell()
    pack(drop)
    drop_across, drop_along = copies(drop)
    send(*drop_across, *drop_along)
    shift_own(post)
    gather(post)
    shift_own(cot)
    gather(cot)
    shift_own(drop)

    @pl.loop(1, NX - 1)
    def _(x):
        halves = [[without_edge(h, part) for part in first_half(("x", x, h))] for h in range(2)]
        for q in range(3):
            grades[q, x] = halves[0][q] + halves[1][q]

    line = jnp.zeros((8, NZ), jnp.float32)
    for plane in range(NX):
        terms = [grades[q, x] for q, x in enumerate((plane, plane + 1, plane - 1)) if 0 < x < NX - 1]
        line = line + laid(functools.reduce(jnp.add, terms), plane + 1)
    line_ref[...] = line
    arrive(post, cot)
    receive(cot)
    receive(post)

    for end in (0, 1):
        at = (NX - 1) * end
        for h in range(2):
            for q, part in enumerate(first_half(("y", at, h), late(("y", at, h)))):
                kept = jnp.zeros((8, NZ), jnp.float32) if part is None else without_edge(h, part)
                y_grades[end, q, pl.ds(8 * h, 8), :] = kept
    for end in (0, 1):
        at = (NX - 1) * end
        halves = [first_half(("x", at, h), late(("x", at, h))) for h in range(2)]
        for q in range(3):
            both = [part[q] for part in halves if part[q] is not None]
            grades[q, at] = functools.reduce(jnp.add, both) if both else jnp.zeros((8, NZ), jnp.float32)
    pack(pre)
    pre_across, pre_along = copies(pre)
    send(*pre_across, *pre_along)
    arrive(drop)
    receive(drop)
    for end in (0, 1):
        at = (NX - 1) * end
        shares = [rest_of(("x", at, h)) for h in range(2)]
        for q in range(3):
            both = [part[q] for part in shares if part[q] is not None]
            if both:
                grades[q, at] += functools.reduce(jnp.add, both)
        for h in range(2):
            for q, part in enumerate(rest_of(("y", at, h))):
                if part is not None:
                    y_grades[end, q, pl.ds(8 * h, 8), :] += without_edge(h, part)

    line = line_ref[...]
    for q, lead in enumerate((1, 0, 2)):
        for at in (0, NX - 1):
            line = line + laid(grades[q, at], at + lead)
        for h in range(2):
            part = y_grades[0, q, pl.ds(8 * h, 8), :] + y_grades[1, q, pl.ds(8 * h, 8), :]
            line = line + laid(part, row_at + (8 * h + lead))
    rows[0, sp] = jnp.sum(line, axis=0, keepdims=True)
    hear()
    for side, step in peers:
        pltpu.make_async_remote_copy(
            src_ref=rows.at[0, sp],
            dst_ref=rows.at[side, sp],
            send_sem=row_sems.at[0],
            recv_sem=row_sems.at[1],
            device_id=peer(side, step),
        ).start()

    shift_own(pre)

    @pl.loop(1, NX - 1)
    def _(x):
        for h in range(2):
            second_half(("x", x, h))

    arrive(pre)
    receive(pre)

    @pl.loop(0, 2)
    def _(end):
        at = (NX - 1) * end
        for h in range(2):
            second_half(("x", at, h))
        for h in range(2):
            second_half(("y", at, h))

    finish()
    all_rows = rows.reshape(3 * spans, 1, NZ).at[pl.ds(0, len(peers))]
    take(all_rows, row_sems.at[1])
    one_lane = lax.broadcasted_iota(jnp.int32, (1, NZ), 1)
    total = jnp.sum(rows[0], axis=0)
    from_down = jnp.sum(rows[1], axis=0)
    from_up = jnp.sum(rows[2], axis=0)
    total = total + jnp.where(one_lane == 1, pltpu.roll(from_down, NZ - NX, 1), 0.0)
    total = total + jnp.where(one_lane == NX, pltpu.roll(from_up, NX, 1), 0.0)
    total = pltpu.roll(total, NZ - 1, 1) * (1.0 / math.sqrt(spans * NY * NZ))
    profile_ref[...] = total[:, :NX]
    take(all_rows, row_sems.at[0])


def local(flows, spans, populations, gray, fluid_mask, cotangent):
    def vmem(*shape):
        return pltpu.VMEM(shape, jnp.float32)

    zs = len(Z_DIRS)
    adjoint, profile = pl.pallas_call(
        functools.partial(kernel, flows, spans),
        out_shape=(
            jax.ShapeDtypeStruct((19, NX, NY, NZ), jnp.float32),
            jax.ShapeDtypeStruct((1, NX), jnp.float32),
        ),
        in_specs=[pl.BlockSpec(memory_space=pl.ANY)] * 4,
        out_specs=(pl.BlockSpec(memory_space=pltpu.VMEM), pl.BlockSpec(memory_space=pltpu.VMEM)),
        scratch_shapes=[
            vmem(19, NX, NY, NZ),
            vmem(NX, NY, NZ),
            pltpu.VMEM((NX, NY, NZ), jnp.int32),
            vmem(3, NX, NY, NZ),
            *[vmem(19, NX + 2, PITCH, NZ), vmem(zs, NX + 2, PITCH, NZ)] * 4,
            vmem(4, 2, 5, NX, NZ),
            vmem(4, 2, 6, NX, NZ),
            vmem(2, 2, 19, PITCH, NZ),
            vmem(3, NX, 8, NZ),
            vmem(2, 3, NX, NZ),
            vmem(8, NZ),
            vmem(3, spans, 1, NZ),
            pltpu.SemaphoreType.DMA((CHUNKS + 3,)),
            pltpu.SemaphoreType.REGULAR,
            pltpu.SemaphoreType.DMA((3,)),
            pltpu.SemaphoreType.DMA((3, 3)),
            pltpu.SemaphoreType.DMA((2,)),
        ],
        compiler_params=pltpu.CompilerParams(
            collective_id=0, has_side_effects=True, vmem_limit_bytes=44 * 1024 * 1024
        ),
    )(*[pltpu.with_memory_space_constraint(x, pltpu.HBM) for x in (populations, gray, fluid_mask, cotangent)])
    return adjoint, profile.reshape(NX)


def solution(mesh):
    placed = (
        P(None, "flow", "span", None),
        P("flow", "span", None),
        P("flow", "span", None),
        P(None, "flow", "span", None),
    )
    return jax.shard_map(
        functools.partial(local, mesh.shape["flow"], mesh.shape["span"]),
        mesh=mesh,
        in_specs=placed,
        out_specs=(P(None, "flow", "span", None), P("flow")),
        check_vma=False,
    )
```
